128 devices in a mesh: gx: 8 (over z, x_hi), gy: 4 (over y), gz: 4 (over x_lo, core).
Axes of the slice: x: 4 (x_hi: 2, x_lo: 2; x = x_hi * 2 + x_lo), y: 4, z: 4, core: 2. Of those that a mesh axis runs over, the one named last changes fastest.
Arguments:
- tokens: bfloat16 [2048, 4096], P('gx', ('gz', 'gy')), may hold values from -6 to 6
- w_gate: bfloat16 [4096, 11264], P(('gz', 'gx'), 'gy'), may hold values from -0.09375 to 0.09375
- w_up: bfloat16 [4096, 11264], P(('gz', 'gx'), 'gy'), may hold values from -0.09375 to 0.09375
- w_down: bfloat16 [11264, 4096], P(('gy', 'gx'), 'gz'), may hold values from -0.0546875 to 0.0546875
- grad_output: bfloat16 [2048, 4096], P('gx', ('gz', 'gy')), may hold values from -6 to 6
Outputs:
- output: bfloat16 [2048, 4096], P('gx', ('gz', 'gy'))
- grad_input: bfloat16 [2048, 4096], P('gx', ('gz', 'gy'))
- grad_gate: bfloat16 [4096, 11264], P(('gz', 'gx'), 'gy')
- grad_up: bfloat16 [4096, 11264], P(('gz', 'gx'), 'gy')
- grad_down: bfloat16 [11264, 4096], P(('gy', 'gx'), 'gz')
The draws below stay inside these ranges and needn't reach their ends.
All inputs are finite; a program needn't handle non-finite values.
Results may differ from the reference program's by a relative error of at most 0.029.
Values may be sent and summed in bfloat16 or wider, within the bound.
No kernel may reach another device: no remote copies, remote signals or barrier semaphores. Data moves between devices by JAX's collectives and lax.ppermute only.
A program may use at most 128 MiB of HBM per device.

```python
import math
import jax
import jax.numpy as jnp
from jax import lax

D = 4096
FF = 11264
TOK_ROW = 256
TOKENS = 2048


def block_levels(key, shape, pieces, least, largest):
    level, own = 1.0, jax.random.fold_in(key, 6)
    for dim, parts in pieces:
        heights = jnp.exp(jax.random.uniform(jax.random.fold_in(own, dim), (parts,), jnp.float32, least / len(pieces), largest / len(pieces)))
        level = level * jnp.repeat(heights, shape[dim] // parts).reshape([-1 if axis == dim else 1 for axis in range(len(shape))])
    return level


def normal_values(stream_key, extent, width, most, split=(), dtype=jnp.bfloat16):
    gain = block_levels(stream_key, extent, split, -0.22, 0.18) if split else 1.0
    array = jax.random.normal(stream_key, extent, jnp.float32) * width * gain
    return jnp.minimum(jnp.maximum(array, -most), most).astype(dtype)


def setup_inputs(seed: int = 0) -> dict:
    streams_of = jax.random.split(jax.random.key(seed), 6)
    tokens = normal_values(streams_of[0], (TOKENS, D), 1.0, 6.0, ((0, 8), (1, 16)))
    w_gate = normal_values(streams_of[1], (D, FF), D ** -0.5, 0.09375, ((0, 32), (1, 4)))
    w_up = normal_values(streams_of[2], (D, FF), D ** -0.5, 0.09375, ((0, 32), (1, 4)))
    w_down = normal_values(streams_of[3], (FF, D), FF ** -0.5, 0.0546875, ((0, 32), (1, 4)))
    grad_output = normal_values(streams_of[4], (TOKENS, D), 1.0, 6.0, ((0, 8), (1, 16)))
    return dict(tokens=tokens, w_gate=w_gate, w_up=w_up, w_down=w_down, grad_output=grad_output)


def blockwise_sum(left_side, right_side, loss_scale):
    block_count = left_side.shape[0] // TOK_ROW
    running = jnp.zeros((left_side.shape[1], right_side.shape[1]), jnp.float32)
    for block_index in range(block_count):
        left_block = left_side[block_index * TOK_ROW:(block_index + 1) * TOK_ROW]
        right_block = right_side[block_index * TOK_ROW:(block_index + 1) * TOK_ROW]
        block_term = jnp.dot(left_block.T, right_block, preferred_element_type=jnp.float32) * loss_scale
        running = running + lax.optimization_barrier(block_term.astype(jnp.bfloat16)).astype(jnp.float32)
    return running.astype(jnp.bfloat16)

def reference(tokens, w_gate, w_up, w_down, grad_output):
    gate_sum = jnp.dot(tokens, w_gate, preferred_element_type=jnp.float32)
    up_sum = jnp.dot(tokens, w_up, preferred_element_type=jnp.float32)
    hidden = (jax.nn.silu(gate_sum) * up_sum).astype(jnp.bfloat16)
    output = jnp.dot(hidden, w_down, preferred_element_type=jnp.float32).astype(jnp.bfloat16)
    grad_hidden = jnp.dot(grad_output, w_down.T, preferred_element_type=jnp.float32)
    sigmoid_gate = jax.nn.sigmoid(gate_sum)
    grad_gate_act = (grad_hidden * up_sum * sigmoid_gate * (1.0 + gate_sum * (1.0 - sigmoid_gate))).astype(jnp.bfloat16)
    grad_up_act = (grad_hidden * gate_sum * sigmoid_gate).astype(jnp.bfloat16)
    grad_input = (jnp.dot(grad_gate_act, w_gate.T, preferred_element_type=jnp.float32) + jnp.dot(grad_up_act, w_up.T, preferred_element_type=jnp.float32)).astype(jnp.bfloat16)
    loss_scale = 1.0 / math.sqrt(tokens.shape[0])
    grad_gate = blockwise_sum(tokens, grad_gate_act, loss_scale)
    grad_up = blockwise_sum(tokens, grad_up_act, loss_scale)
    grad_down = blockwise_sum(hidden, grad_output, loss_scale)
    return (output, grad_input, grad_gate, grad_up, grad_down)
```

```python
import math

import jax
import jax.numpy as jnp
from jax import lax
from jax.sharding import PartitionSpec as P


BF16 = jnp.bfloat16
F32 = jnp.float32


def shift_z(array, steps):
    return lax.ppermute(
        array, "gx", [(i, ((i // 2 + steps) % 4) * 2 + i % 2) for i in range(8)]
    )


def shift_y(array, steps):
    return lax.ppermute(array, "gy", [(i, (i + steps) % 4) for i in range(4)])


def swap_x_hi(array):
    return lax.ppermute(array, "gx", [(i, i ^ 1) for i in range(8)])


def swap_x_lo(array):
    return lax.ppermute(array, "gz", [(i, i ^ 2) for i in range(4)])


def swap_core(array):
    return lax.ppermute(array, "gz", [(i, i ^ 1) for i in range(4)])


def rows_at(array, index, count):
    return lax.dynamic_slice_in_dim(array, index * count, count, axis=0)


def columns_at(array, index, count):
    return lax.dynamic_slice_in_dim(array, index * count, count, axis=1)


def ordered_rows(first, mine, other):
    return jnp.where(
        first, jnp.concatenate([mine, other], axis=0), jnp.concatenate([other, mine], axis=0)
    )


def gather_columns(block, y):
    count = block.shape[1]
    whole = jnp.zeros((block.shape[0], 4 * count), block.dtype)
    pieces = [block] + [shift_y(block, k) for k in (1, 3, 2)]
    for k, piece in zip((0, 1, 3, 2), pieces):
        whole = lax.dynamic_update_slice_in_dim(whole, piece, ((y - k) % 4) * count, axis=1)
    return whole


def scatter_columns(part, y):
    count = part.shape[1] // 4
    total = columns_at(part, y, count).astype(F32)
    for k in (1, 3, 2):
        total = total + shift_y(columns_at(part, (y + k) % 4, count), k).astype(F32)
    return total


def scatter_gz(part, x_lo, core):
    half = part.shape[0] // 2
    part = (
        rows_at(part, core, half).astype(F32)
        + swap_core(rows_at(part, 1 - core, half)).astype(F32)
    ).astype(BF16)
    return rows_at(part, x_lo, half // 2).astype(F32) + swap_x_lo(
        rows_at(part, 1 - x_lo, half // 2)
    ).astype(F32)


def gather_gz(block, x_lo, core):
    block = ordered_rows(x_lo == 0, block, swap_x_lo(block))
    return ordered_rows(core == 0, block, swap_core(block))


def dot(left_side, right_side, left_dim, right_dim):
    return lax.dot_general(
        left_side,
        right_side,
        (((left_dim,), (right_dim,)), ((), ())),
        preferred_element_type=F32,
    )


PEERS = tuple((k, h) for k in (1, 3, 2, 0) for h in (0, 1) if (k, h) != (0, 0))


def exchange_gx(pieces, gx):
    z, x_hi = gx // 2, gx % 2
    result = lax.dynamic_update_index_in_dim(
        jnp.zeros_like(pieces), lax.dynamic_index_in_dim(pieces, gx, 0, True), gx, 0
    )
    for k, h in PEERS:
        target = ((z + k) % 4) * 2 + (x_hi ^ h)
        source = ((z - k) % 4) * 2 + (x_hi ^ h)
        piece = lax.ppermute(
            lax.dynamic_index_in_dim(pieces, target, 0, True),
            "gx",
            [(i, ((i // 2 + k) % 4) * 2 + ((i % 2) ^ h)) for i in range(8)],
        )
        result = lax.dynamic_update_index_in_dim(result, piece, source, 0)
    return result


def on_device(tokens, w_gate, w_up, w_down, grad_output):
    gx, y, gz = lax.axis_index("gx"), lax.axis_index("gy"), lax.axis_index("gz")
    x_lo, core = gz // 2, gz % 2
    tok_rows = tokens.shape[0]
    rows_in, width_hidden = w_gate.shape
    own = width_hidden // 8
    loss_scale = 1.0 / math.sqrt(tok_rows * 8)

    pieces = jnp.concatenate(
        [w_gate.reshape(rows_in, 8, own), w_up.reshape(rows_in, 8, own)], axis=2
    ).transpose(1, 0, 2)
    w_pair = exchange_gx(pieces, gx).reshape(8 * rows_in, 2 * own)

    block = gather_columns(tokens, y)
    block = jnp.concatenate([block, swap_x_hi(block)], axis=0)
    chunks = [block] + [shift_z(block, k) for k in (1, 3, 2)]

    block = jnp.concatenate([grad_output, swap_x_hi(grad_output)], axis=0)
    grad_chunks = [block] + [shift_z(block, k) for k in (1, 3, 2)]
    grad_chunks = [gather_columns(piece, y) for piece in grad_chunks]

    hidden_chunks, act_chunks = [], []
    output_parts, input_parts = [], []
    for chunk, grad_chunk in zip(chunks, grad_chunks):
        pair = scatter_gz(dot(chunk, w_pair, 1, 0).astype(BF16), x_lo, core)
        grad_hidden = scatter_gz(dot(grad_chunk, w_down, 1, 1).astype(BF16), x_lo, core)
        gate_sum, up_sum = pair[:, :own], pair[:, own:]
        sigmoid_gate = jax.nn.sigmoid(gate_sum)
        hidden = (gate_sum * sigmoid_gate * up_sum).astype(BF16)
        grad_gate_act = (
            grad_hidden * up_sum * sigmoid_gate * (1.0 + gate_sum * (1.0 - sigmoid_gate))
        ).astype(BF16)
        grad_up_act = (grad_hidden * gate_sum * sigmoid_gate).astype(BF16)
        hidden = gather_gz(hidden, x_lo, core)
        acts = gather_gz(jnp.concatenate([grad_gate_act, grad_up_act], axis=1), x_lo, core)
        hidden_chunks.append(hidden)
        act_chunks.append(acts)
        output_parts.append(dot(hidden, w_down, 1, 0).astype(BF16))
        input_parts.append(dot(acts, w_pair, 1, 1).astype(BF16))

    all_tokens = jnp.concatenate(chunks, axis=0)
    all_acts = jnp.concatenate(act_chunks, axis=0)
    grad_pair = (dot(all_tokens, all_acts, 0, 0) * loss_scale).astype(BF16)
    grad_pair = exchange_gx(grad_pair.reshape(8, rows_in, 2 * own), gx)
    grad_pair = grad_pair.transpose(1, 0, 2)
    grad_gate = grad_pair[:, :, :own].reshape(rows_in, width_hidden)
    grad_up = grad_pair[:, :, own:].reshape(rows_in, width_hidden)
    all_hidden = jnp.concatenate(hidden_chunks, axis=0)
    all_grads = jnp.concatenate(grad_chunks, axis=0)
    grad_down = (dot(all_hidden, all_grads, 0, 0) * loss_scale).astype(BF16)

    total = output_parts[0].astype(F32)
    for k, part in zip((1, 3, 2), output_parts[1:]):
        total = total + shift_z(part, -k).astype(F32)
    total = total.astype(BF16)
    total = (total[:tok_rows].astype(F32) + swap_x_hi(total[tok_rows:]).astype(F32)).astype(BF16)
    output = scatter_columns(total, y).astype(BF16)

    sums = [scatter_columns(part, y).astype(BF16) for part in input_parts]
    total = sums[0].astype(F32)
    for k, part in zip((1, 3, 2), sums[1:]):
        total = total + shift_z(part, -k).astype(F32)
    total = total.astype(BF16)
    grad_input = (
        total[:tok_rows].astype(F32) + swap_x_hi(total[tok_rows:]).astype(F32)
    ).astype(BF16)
    return (output, grad_input, grad_gate, grad_up, grad_down)


def solution(mesh):
    placed = (
        P("gx", ("gz", "gy")),
        P(("gz", "gx"), "gy"),
        P(("gz", "gx"), "gy"),
        P(("gy", "gx"), "gz"),
        P("gx", ("gz", "gy")),
    )
    return jax.shard_map(
        on_device,
        mesh=mesh,
        in_specs=placed,
        out_specs=(
            P("gx", ("gz", "gy")),
            P("gx", ("gz", "gy")),
            P(("gz", "gx"), "gy"),
            P(("gz", "gx"), "gy"),
            P(("gy", "gx"), "gz"),
        ),
        check_vma=False,
    )
```

```python
import functools
import math

import jax
import jax.numpy as jnp
from jax import lax
from jax.experimental import pallas as pl
from jax.experimental.pallas import tpu as pltpu
from jax.sharding import PartitionSpec as P


BF16 = jnp.bfloat16
F32 = jnp.float32
LANES = 128


def shift_z(array, steps):
    return lax.ppermute(
        array, "gx", [(i, ((i // 2 + steps) % 4) * 2 + i % 2) for i in range(8)]
    )


def shift_y(array, steps):
    return lax.ppermute(array, "gy", [(i, (i + steps) % 4) for i in range(4)])


def swap_x_hi(array):
    return lax.ppermute(array, "gx", [(i, i ^ 1) for i in range(8)])


def swap_x_lo(array):
    return lax.ppermute(array, "gz", [(i, i ^ 2) for i in range(4)])


def swap_x(array):
    return lax.ppermute(array, ("gx", "gz"), [(i, i ^ 6) for i in range(32)])


def swap_core(array):
    return lax.ppermute(array, "gz", [(i, i ^ 1) for i in range(4)])


def add(left_side, right_side):
    return left_side.astype(F32) + right_side.astype(F32)


def dot(left_side, right_side, left_dim, right_dim):
    return lax.dot_general(
        left_side,
        right_side,
        (((left_dim,), (right_dim,)), ((), ())),
        preferred_element_type=F32,
    )


class Operand:
    def __init__(self, source, held, semaphore):
        self.copy = pltpu.make_async_copy(source, held, semaphore)
        self.copy.start()
        self.held = held
        self.shape = held.shape

    def ready(self):
        if self.copy is not None:
            self.copy.wait()
            self.copy = None
        return self.held

    def __getitem__(self, index):
        return self.ready()[index]


def local_call(kernel, out_shapes, operands, scratch_shapes=(), vmem=40):
    count, outs = len(operands), len(out_shapes)

    def body(*refs):
        sources, refs = refs[:count], refs[count:]
        results, refs = refs[:outs], refs[outs:]
        held, semaphores, scratch = refs[:count], refs[count], refs[count + 1 :]
        inputs = [
            Operand(source, place, semaphores.at[i])
            for i, (source, place) in enumerate(zip(sources, held))
        ]
        kernel(*inputs, *results, *scratch)
        for operand in inputs:
            operand.ready()

    return list(
        pl.pallas_call(
            body,
            out_shape=[jax.ShapeDtypeStruct(shape, BF16) for shape in out_shapes],
            in_specs=[pl.BlockSpec(memory_space=pl.ANY)] * count,
            out_specs=[pl.BlockSpec(memory_space=pltpu.VMEM)] * outs,
            scratch_shapes=[
                *(pltpu.VMEM(array.shape, BF16) for array in operands),
                pltpu.SemaphoreType.DMA((count,)),
                *scratch_shapes,
            ],
            compiler_params=pltpu.CompilerParams(vmem_limit_bytes=vmem * 2**20),
        )(*operands)
    )


def assembled_call(kernel, out_shapes, operands, buffers, copies, vmem=40):
    count, outs = len(operands), len(out_shapes)

    def body(*refs):
        sources, refs = refs[:count], refs[count:]
        results, (*held, semaphores) = refs[:outs], refs[outs:]
        started = []

        def copy(source, target):
            started.append(pltpu.make_async_copy(source, target, semaphores.at[len(started)]))
            started[-1].start()
            return started[-1]

        kernel(copy, sources, results, *held)

    return list(
        pl.pallas_call(
            body,
            out_shape=[jax.ShapeDtypeStruct(shape, BF16) for shape in out_shapes],
            in_specs=[pl.BlockSpec(memory_space=pl.ANY)] * count,
            out_specs=[pl.BlockSpec(memory_space=pltpu.VMEM)] * outs,
            scratch_shapes=[
                *(pltpu.VMEM(shape, BF16) for shape in buffers),
                pltpu.SemaphoreType.DMA((copies,)),
            ],
            compiler_params=pltpu.CompilerParams(vmem_limit_bytes=vmem * 2**20),
        )(*operands)
    )


def wait_all(copies):
    for copy in copies:
        copy.wait()


def after(array, *earlier):
    return lax.optimization_barrier((array, *earlier))[0]


def core_index():
    return lax.rem(lax.axis_index("gz"), 2)


def x_lo_index():
    return lax.div(lax.axis_index("gz"), 2)


def block(index, count):
    return pl.ds(pl.multiple_of(index * count, count), count)


def feature_block(k, count):
    return block(lax.rem(lax.axis_index("gy") + (4 - k), 4), count)


def split_rows(tokens, grads, mine, theirs):
    half, count = mine.shape[0], tokens.shape[1]
    for out, index in ((mine, x_lo_index()), (theirs, 1 - x_lo_index())):
        out[:, :count] = tokens[block(index, half)]
        out[:, count:] = grads[block(index, half)]


def arrange_rows(near, far, near_x, far_x, tokens, grads):
    half, count = near.shape[0], near.shape[1] // 2
    core = core_index()
    for index, left, right in ((core, near, far), (1 - core, near_x, far_x)):
        tokens[block(index, half), :count] = left[:, :count]
        tokens[block(index, half), count:] = right[:, :count]
        grads[block(index, half), :count] = left[:, count:]
        grads[block(index, half), count:] = right[:, count:]


def split_pair(w_gate, w_up, out):
    groups, own = out.shape[0], out.shape[1] // 2
    for first, array in ((0, w_gate), (own, w_up)):
        for g in range(groups):
            out[g, first : first + own] = array[:, g * own : (g + 1) * own].T


def join_blocks(pieces, out):
    groups, own, _ = pieces.shape
    for g in range(groups):
        out[:, g * own : (g + 1) * own] = pieces[g].T


def join_features(*refs):
    *blocks, out = refs
    count, features = blocks[0].shape[1] // 2, out.shape[1] // 2
    for k, part in enumerate(blocks):
        place = lax.rem(lax.axis_index("gy") + (4 - k), 4) * count
        out[:, pl.ds(pl.multiple_of(place, count), count)] = part[:, :count]
        out[:, pl.ds(pl.multiple_of(features + place, count), count)] = part[:, count:]


def pick_features(whole, *outs):
    count, features = outs[0].shape[1] // 2, whole.shape[1] // 2
    for k, out in enumerate(outs):
        place = lax.rem(lax.axis_index("gy") + (4 - k), 4) * count
        out[:, :count] = whole[:, pl.ds(pl.multiple_of(place, count), count)]
        out[:, count:] = whole[:, pl.ds(pl.multiple_of(features + place, count), count)]


def own_place(k, count):
    return lax.rem(lax.axis_index("gy") + (4 - k), 4) * count


def copy_tokens(copy, refs, held):
    copies, first = [], 0
    for ref in refs:
        copies.append(copy(ref, held.at[pl.ds(first, ref.shape[0])]))
        first += ref.shape[0]
    return copies


def copy_grads(copy, refs, held):
    copies = []
    count, features = refs[0].shape[1] // 2, held.shape[1] // 2
    for ref, k, first in zip(refs, (0, 1, 2, 2, 3), (0, 0, 0, refs[2].shape[0], 0)):
        for side in (0, 1):
            place = side * features + own_place(k, count)
            target = held.at[
                pl.ds(first, ref.shape[0]), pl.ds(pl.multiple_of(place, count), count)
            ]
            copies.append(copy(ref.at[:, pl.ds(side * count, count)], target))
    return copies


def copy_pair(copy, near, far, held):
    copies = []
    groups, _, count = near.shape
    for side, ref in enumerate((near, far)):
        for g in range(groups):
            target = held.at[:, pl.ds((side * groups + g) * count, count)]
            copies.append(copy(ref.at[g], target))
    return copies


def copy_down(copy, near, far, held):
    features = near.shape[1]
    return [
        copy(ref, held.at[:, pl.ds(side * features, features)])
        for side, ref in enumerate((near, far))
    ]


def copy_part(copy, mine, other, first, held):
    rows, width = mine.shape[1], held.shape[1]
    return [
        copy(
            ref.at[i, :, pl.ds(first, width)], held.at[pl.ds((2 * i + side) * rows, rows)]
        )
        for i in range(mine.shape[0])
        for side, ref in enumerate((mine, other))
    ]


def sums_products(copy, sources, results, tokens, grads, pair, down):
    keep, send = results
    half, width = keep.shape[1], keep.shape[2] // 3
    own = down.shape[0]
    copies = copy_tokens(copy, sources[:5], tokens)
    copies += copy_pair(copy, *sources[10:12], pair)
    later = copy_grads(copy, sources[5:10], grads) + copy_down(copy, *sources[12:], down)
    padding = jnp.zeros((half, width - own), BF16)
    wait_all(copies)
    for step, (left, right) in enumerate(((tokens, pair), (grads, down))):
        if step == 1:
            wait_all(later)
        for i in (0, 2):
            part = dot(left[pl.ds(2 * i * half, 4 * half)], right[...], 1, 1).astype(BF16)
            for j in (0, 1):
                for out, at in ((keep, 2 * j * half), (send, (2 * j + 1) * half)):
                    rows = part[at : at + half]
                    for k in (0, 1) if step == 0 else (2,):
                        first = k * own if step == 0 else 0
                        out[i + j, :, k * width : k * width + own] = rows[:, first : first + own]
                        out[i + j, :, k * width + own : (k + 1) * width] = padding


def activate(keep, got, out):
    width = out.shape[2] // 3
    for i in range(out.shape[0]):
        gate_sum, up_sum, grad_hidden = (
            add(keep[i, :, k * width : (k + 1) * width], got[i, :, k * width : (k + 1) * width])
            for k in range(3)
        )
        sigmoid_gate = jax.nn.sigmoid(gate_sum)
        out[i, :, :width] = (gate_sum * sigmoid_gate * up_sum).astype(BF16)
        out[i, :, width : 2 * width] = (
            grad_hidden * up_sum * sigmoid_gate * (1.0 + gate_sum * (1.0 - sigmoid_gate))
        ).astype(BF16)
        out[i, :, 2 * width :] = (grad_hidden * gate_sum * sigmoid_gate).astype(BF16)


def output_products(copy, sources, results, hidden, down):
    copies = copy_part(copy, sources[0], sources[1], 0, hidden)
    wait_all(copies + copy_down(copy, *sources[2:], down))
    own, first = down.shape[0], 0
    for out in results:
        rows = out.shape[0]
        out[...] = dot(hidden[pl.ds(first, rows), :own], down[...], 1, 0).astype(BF16)
        first += rows


def input_products(copy, sources, results, acts, pair):
    width, own = acts.shape[1] // 2, pair.shape[0] // 2
    copies = copy_part(copy, sources[0], sources[1], width, acts)
    wait_all(copies + copy_pair(copy, *sources[2:], pair))
    count, features = results[0].shape[1] // 2, pair.shape[1] // 2
    for out, k, first in zip(results, (0, 1, 2, 2, 3), (0, 0, 0, results[2].shape[0], 0)):
        rows = pl.ds(first, out.shape[0])
        for side in (0, 1):
            place = pl.ds(pl.multiple_of(side * features + own_place(k, count), count), count)
            part = dot(acts[rows, :own], pair[:own, place], 1, 0)
            part += dot(acts[rows, width : width + own], pair[own:, place], 1, 0)
            out[:, side * count : (side + 1) * count] = part.astype(BF16)


def pair_gradients(scale, part, copy, sources, results, tokens, acts):
    width = acts.shape[1]
    copies = copy_tokens(copy, sources[:5], tokens)
    wait_all(copies + copy_part(copy, *sources[5:], part * width, acts))
    near, far = results
    groups, own, count = near.shape
    features = groups * count
    for out, first in ((far, features), (near, 0)):
        total = dot(acts[:, :own], tokens[:, pl.ds(first, features)], 0, 0) * scale
        for g in range(groups):
            out[g] = total[:, g * count : (g + 1) * count].astype(BF16)


def down_gradients(scale, copy, sources, results, grads, hidden):
    copies = copy_grads(copy, sources[:5], grads)
    wait_all(copies + copy_part(copy, *sources[5:], 0, hidden))
    near, far = results
    own, features = near.shape
    for out, first in ((far, features), (near, 0)):
        total = dot(hidden[:, :own], grads[:, pl.ds(first, features)], 0, 0)
        out[...] = (total * scale).astype(BF16)


def split_result(output, grad_input, near, far, near_x, far_x):
    half, count = near.shape[0], near.shape[1] // 2
    core = core_index()
    for index, left, right in ((core, near, far), (1 - core, near_x, far_x)):
        for first, array in ((0, output), (count, grad_input)):
            rows = array[block(index, half)]
            left[:, first : first + count] = rows[:, :count]
            right[:, first : first + count] = rows[:, count:]


def join_result(mine, theirs, output, grad_input):
    half, count = mine.shape[0], mine.shape[1] // 2
    for rows, index in ((mine, x_lo_index()), (theirs, 1 - x_lo_index())):
        output[block(index, half)] = rows[:, :count]
        grad_input[block(index, half)] = rows[:, count:]


def ring_gather(shift, array):
    half = array.shape[0] // 2
    before, after = shift(array, 1), shift(array, -1)
    return [array, before, shift(before[:half], 1), shift(after[half:], -1), after]


def ring_scatter(shift, own, before, low, high, after):
    half = low.shape[0]
    from_before, from_after = shift(low, 1), shift(high, -1)
    after = lax.dynamic_update_slice(after, add(after[:half], from_before).astype(BF16), (0, 0))
    before = lax.dynamic_update_slice(
        before, add(before[half:], from_after).astype(BF16), (half, 0)
    )
    return own.astype(F32) + shift(after, 1).astype(F32) + shift(before, -1).astype(F32)


def direct_gather(shift, array):
    return [array, shift(array, 1), shift(array, 2), shift(array, -1)]


def direct_scatter(shift, own, before, opposite, after):
    return (
        own.astype(F32)
        + shift(after, 1).astype(F32)
        + shift(before, -1).astype(F32)
        + shift(opposite, 2).astype(F32)
    )


def on_device(tokens, w_gate, w_up, w_down, grad_output):
    tok_rows, tok_columns = tokens.shape
    rows_in, width_hidden = w_gate.shape
    own = width_hidden // 8
    width = -(-own // LANES) * LANES
    features = 8 * rows_in
    loss_scale = 1.0 / math.sqrt(tok_rows * 8)
    rows, columns = tok_rows // 2, 2 * tok_columns

    mine, theirs = local_call(split_rows, [(rows, columns)] * 2, [tokens, grad_output])
    four = [mine, swap_x_lo(theirs), swap_x_hi(mine), swap_x(theirs)]
    t_block, g_block = local_call(arrange_rows, [(2 * rows, columns)] * 2, four)

    (pieces,) = local_call(split_pair, [(8, 2 * own, rows_in)], [w_gate, w_up])
    pieces, w_down = lax.optimization_barrier((pieces, w_down, *four))[:2]
    w_near = lax.all_to_all(pieces, "gx", 0, 0, tiled=True)
    d_near, d_far = w_down, swap_x_lo(w_down)
    w_far = swap_x_lo(after(w_near, d_far))

    (t_own,) = local_call(
        join_features, [(2 * rows, 2 * features)], direct_gather(shift_y, t_block)
    )
    g_own = jnp.concatenate(direct_gather(shift_z, g_block), axis=0)
    t_own, g_own = lax.optimization_barrier((t_own, g_own))
    t_all = ring_gather(shift_z, t_own)
    g_all = ring_gather(shift_y, g_own)

    all_tokens, all_features = 8 * rows, 2 * features
    whole = (all_tokens, all_features)
    keep, send = assembled_call(
        sums_products,
        [(4, rows, 3 * width)] * 2,
        [*t_all, *g_all, w_near, w_far, d_near, d_far],
        [whole, whole, (2 * own, all_features), (own, all_features)],
        33,
    )
    (mine,) = local_call(activate, [(4, rows, 3 * width)], [keep, swap_core(send)])
    both = [mine, swap_core(mine)]

    grad_pair = []
    for part in (1, 2):
        near, far = assembled_call(
            functools.partial(pair_gradients, loss_scale, part),
            [(8, own, rows_in)] * 2,
            [*t_all, *both],
            [whole, (all_tokens, width)],
            13,
        )
        total = add(near, swap_x_lo(far)).astype(BF16)
        total = lax.all_to_all(total, "gx", 0, 0, tiled=True)
        grad_pair += local_call(join_blocks, [(rows_in, width_hidden)], [total])
        if part == 1:
            both[1] = after(both[1], near)
    near, far = assembled_call(
        functools.partial(down_gradients, loss_scale),
        [(own, features)] * 2,
        [*g_all, *both],
        [whole, (all_tokens, width)],
        18,
    )
    grad_down = add(near, swap_x_lo(far)).astype(BF16)

    shape, half_shape = (2 * rows, all_features), (rows, all_features)
    parts = assembled_call(
        output_products,
        [shape, shape, half_shape, half_shape, shape],
        [*both, d_near, d_far],
        [(all_tokens, width), (own, all_features)],
        10,
    )
    output = ring_scatter(shift_z, *parts).astype(BF16)
    shape, half_shape = (all_tokens, columns), (all_tokens // 2, columns)
    parts = assembled_call(
        input_products,
        [shape, shape, half_shape, half_shape, shape],
        [*both, w_near, w_far],
        [(all_tokens, 2 * width), (2 * own, all_features)],
        24,
    )
    grad_input = ring_scatter(shift_y, *parts).astype(BF16)
    parts = local_call(pick_features, [(2 * rows, columns)] * 4, [output])
    output = direct_scatter(shift_y, *parts).astype(BF16)
    parts = [grad_input[2 * k * rows : 2 * (k + 1) * rows] for k in range(4)]
    grad_input = direct_scatter(shift_z, *parts).astype(BF16)
    near, far, near_x, far_x = local_call(
        split_result, [(rows, columns)] * 4, [output, grad_input]
    )
    mine = add(near, swap_x_hi(near_x)).astype(BF16)
    theirs = add(swap_x_lo(far), swap_x(far_x)).astype(BF16)
    output, grad_input = local_call(join_result, [tokens.shape] * 2, [mine, theirs])
    return (output, grad_input, *grad_pair, grad_down)


def solution(mesh):
    placed = (
        P("gx", ("gz", "gy")),
        P(("gz", "gx"), "gy"),
        P(("gz", "gx"), "gy"),
        P(("gy", "gx"), "gz"),
        P("gx", ("gz", "gy")),
    )
    return jax.shard_map(
        on_device,
        mesh=mesh,
        in_specs=placed,
        out_specs=(
            P("gx", ("gz", "gy")),
            P("gx", ("gz", "gy")),
            P(("gz", "gx"), "gy"),
            P(("gz", "gx"), "gy"),
            P(("gy", "gx"), "gz"),
        ),
        check_vma=False,
    )
```

```python
import functools
import math

import jax
import jax.numpy as jnp
from jax import lax
from jax.experimental import pallas as pl
from jax.experimental.pallas import tpu as pltpu
from jax.sharding import PartitionSpec as P


BF16 = jnp.bfloat16
F32 = jnp.float32
LANES = 128


def shift_z(array, steps):
    return lax.ppermute(
        array, "gx", [(i, ((i // 2 + steps) % 4) * 2 + i % 2) for i in range(8)]
    )


def shift_y(array, steps):
    return lax.ppermute(array, "gy", [(i, (i + steps) % 4) for i in range(4)])


def swap_x_hi(array):
    return lax.ppermute(array, "gx", [(i, i ^ 1) for i in range(8)])


def swap_x_lo(array):
    return lax.ppermute(array, "gz", [(i, i ^ 2) for i in range(4)])


def swap_x(array):
    return lax.ppermute(array, ("gx", "gz"), [(i, i ^ 6) for i in range(32)])


def swap_core(array):
    return lax.ppermute(array, "gz", [(i, i ^ 1) for i in range(4)])


def add(left_side, right_side):
    return left_side.astype(F32) + right_side.astype(F32)


def dot(left_side, right_side, left_dim, right_dim):
    return lax.dot_general(
        left_side,
        right_side,
        (((left_dim,), (right_dim,)), ((), ())),
        preferred_element_type=F32,
    )


class Operand:
    def __init__(self, source, held, semaphore):
        self.copy = pltpu.make_async_copy(source, held, semaphore)
        self.copy.start()
        self.held = held
        self.shape = held.shape

    def ready(self):
        if self.copy is not None:
            self.copy.wait()
            self.copy = None
        return self.held

    def __getitem__(self, index):
        return self.ready()[index]


def local_call(kernel, out_shapes, operands, scratch_shapes=(), vmem=40):
    count, outs = len(operands), len(out_shapes)

    def body(*refs):
        sources, refs = refs[:count], refs[count:]
        results, refs = refs[:outs], refs[outs:]
        held, semaphores, scratch = refs[:count], refs[count], refs[count + 1 :]
        inputs = [
            Operand(source, place, semaphores.at[i])
            for i, (source, place) in enumerate(zip(sources, held))
        ]
        kernel(*inputs, *results, *scratch)
        for operand in inputs:
            operand.ready()

    return list(
        pl.pallas_call(
            body,
            out_shape=[jax.ShapeDtypeStruct(shape, BF16) for shape in out_shapes],
            in_specs=[pl.BlockSpec(memory_space=pl.ANY)] * count,
            out_specs=[pl.BlockSpec(memory_space=pltpu.VMEM)] * outs,
            scratch_shapes=[
                *(pltpu.VMEM(array.shape, BF16) for array in operands),
                pltpu.SemaphoreType.DMA((count,)),
                *scratch_shapes,
            ],
            compiler_params=pltpu.CompilerParams(vmem_limit_bytes=vmem * 2**20),
        )(*operands)
    )


def assembled_call(kernel, out_shapes, operands, buffers, copies, vmem=40, dtype=BF16):
    count, outs = len(operands), len(out_shapes)
    buffers = [buffer if len(buffer) == 2 and isinstance(buffer[0], tuple) else (buffer, BF16) for buffer in buffers]

    def body(*refs):
        sources, refs = refs[:count], refs[count:]
        results, (*held, semaphores) = refs[:outs], refs[outs:]
        started = []

        def copy(source, target):
            started.append(pltpu.make_async_copy(source, target, semaphores.at[len(started)]))
            started[-1].start()
            return started[-1]

        kernel(copy, sources, results, *held)

    return list(
        pl.pallas_call(
            body,
            out_shape=[jax.ShapeDtypeStruct(shape, dtype) for shape in out_shapes],
            in_specs=[pl.BlockSpec(memory_space=pl.ANY)] * count,
            out_specs=[pl.BlockSpec(memory_space=pltpu.VMEM)] * outs,
            scratch_shapes=[
                *(pltpu.VMEM(*buffer) for buffer in buffers),
                pltpu.SemaphoreType.DMA((copies,)),
            ],
            compiler_params=pltpu.CompilerParams(vmem_limit_bytes=vmem * 2**20),
        )(*operands)
    )


def wait_all(copies):
    for copy in copies:
        copy.wait()


def after(array, *earlier):
    return lax.optimization_barrier((array, *earlier))[0]


def core_index():
    return lax.rem(lax.axis_index("gz"), 2)


def x_lo_index():
    return lax.div(lax.axis_index("gz"), 2)


def block(index, count):
    return pl.ds(pl.multiple_of(index * count, count), count)


def feature_block(k, count):
    return block(lax.rem(lax.axis_index("gy") + (4 - k), 4), count)


def split_rows(tokens, grads, mine, theirs):
    half, count = mine.shape[0], tokens.shape[1]
    for out, index in ((mine, x_lo_index()), (theirs, 1 - x_lo_index())):
        out[:, :count] = tokens[block(index, half)]
        out[:, count:] = grads[block(index, half)]


def arrange_rows(near, far, near_x, far_x, tokens, grads):
    half, count = near.shape[0], near.shape[1] // 2
    core = core_index()
    for index, left, right in ((core, near, far), (1 - core, near_x, far_x)):
        tokens[block(index, half), :count] = left[:, :count]
        tokens[block(index, half), count:] = right[:, :count]
        grads[block(index, half), :count] = left[:, count:]
        grads[block(index, half), count:] = right[:, count:]


def split_pair(w_gate, w_up, out):
    groups, own = out.shape[0], out.shape[1] // 2
    for first, array in ((0, w_gate), (own, w_up)):
        for g in range(groups):
            out[g, first : first + own] = array[:, g * own : (g + 1) * own].T


def join_blocks(pieces, gate, up):
    groups, both, _ = pieces.shape
    own = both // 2
    for g in range(groups):
        gate[:, g * own : (g + 1) * own] = pieces[g, :own].T
        up[:, g * own : (g + 1) * own] = pieces[g, own:].T


def join_features(*refs):
    *blocks, out = refs
    count, features = blocks[0].shape[1] // 2, out.shape[1] // 2
    for k, part in enumerate(blocks):
        place = lax.rem(lax.axis_index("gy") + (4 - k), 4) * count
        out[:, pl.ds(pl.multiple_of(place, count), count)] = part[:, :count]
        out[:, pl.ds(pl.multiple_of(features + place, count), count)] = part[:, count:]


def pick_features(whole, *outs):
    count, features = outs[0].shape[1] // 2, whole.shape[1] // 2
    for k, out in enumerate(outs):
        place = lax.rem(lax.axis_index("gy") + (4 - k), 4) * count
        out[:, :count] = whole[:, pl.ds(pl.multiple_of(place, count), count)]
        out[:, count:] = whole[:, pl.ds(pl.multiple_of(features + place, count), count)]


def own_place(k, count):
    return lax.rem(lax.axis_index("gy") + (4 - k), 4) * count


def copy_tokens(copy, refs, held):
    copies, first = [], 0
    for ref in refs:
        copies.append(copy(ref, held.at[pl.ds(first, ref.shape[0])]))
        first += ref.shape[0]
    return copies


def copy_grads(copy, refs, held):
    copies = []
    count, features = refs[0].shape[1] // 2, held.shape[1] // 2
    for ref, k, first in zip(refs, (0, 1, 2, 2, 3), (0, 0, 0, refs[2].shape[0], 0)):
        for side in (0, 1):
            place = side * features + own_place(k, count)
            target = held.at[
                pl.ds(first, ref.shape[0]), pl.ds(pl.multiple_of(place, count), count)
            ]
            copies.append(copy(ref.at[:, pl.ds(side * count, count)], target))
    return copies


def copy_blocks(copy, ref, held):
    groups, _, count = ref.shape
    return [copy(ref.at[g], held.at[:, pl.ds(g * count, count)]) for g in range(groups)]


def copy_pair(copy, near, far, held):
    features = held.shape[1] // 2
    copies = copy_blocks(copy, near, held.at[:, pl.ds(0, features)])
    return copies + copy_blocks(copy, far, held.at[:, pl.ds(features, features)])


def copy_down(copy, near, far, held):
    features = near.shape[1]
    return [
        copy(ref, held.at[:, pl.ds(side * features, features)])
        for side, ref in enumerate((near, far))
    ]


def copy_part(copy, mine, other, first, held):
    rows, width = mine.shape[1], held.shape[1]
    return [
        copy(
            ref.at[i, :, pl.ds(first, width)], held.at[pl.ds((2 * i + side) * rows, rows)]
        )
        for i in range(mine.shape[0])
        for side, ref in enumerate((mine, other))
    ]


def near_products(copy, sources, results, tokens, pair):
    features = tokens.shape[1]
    copies = copy_blocks(copy, sources[5], pair)
    copies += copy_tokens(copy, [ref.at[:, pl.ds(0, features)] for ref in sources[:5]], tokens)
    wait_all(copies)
    results[0][...] = dot(tokens[...], pair[...], 1, 1)


def pair_products(copy, sources, results, tokens, pair, share):
    keep, send = results
    half, width = keep.shape[1], keep.shape[2] // 2
    own = pair.shape[0] // 2
    features = tokens.shape[1]
    copies = copy_blocks(copy, sources[5], pair)
    far = [ref.at[:, pl.ds(features, features)] for ref in sources[:5]]
    chunks = copy_tokens(copy, far, tokens)
    rows = 4 * half
    shares = [
        copy(sources[6].at[pl.ds(first, rows)], share.at[pl.ds(first, rows)]) for first in (0, rows)
    ]
    wait_all(copies)
    padding = jnp.zeros((half, width - own), BF16)
    for i, arrived in ((0, chunks[:2]), (2, chunks[2:])):
        here = pl.ds(2 * i * half, rows)
        wait_all(arrived)
        part = dot(tokens[here], pair[...], 1, 1)
        shares[i // 2].wait()
        part = (part + share[here]).astype(BF16)
        for j in (0, 1):
            for out, at in ((keep, 2 * j * half), (send, (2 * j + 1) * half)):
                piece = part[at : at + half]
                for k in (0, 1):
                    out[i + j, :, k * width : k * width + own] = piece[:, k * own : (k + 1) * own]
                    out[i + j, :, k * width + own : (k + 1) * width] = padding


def hidden_products(copy, sources, results, grads, down):
    keep, send = results
    half, width = keep.shape[1:]
    own = down.shape[0]
    copies = copy_down(copy, *sources[5:], down)
    wait_all(copies + copy_grads(copy, sources[:5], grads))
    padding = jnp.zeros((half, width - own), BF16)
    for i in (0, 2):
        part = dot(grads[pl.ds(2 * i * half, 4 * half)], down[...], 1, 1).astype(BF16)
        for j in (0, 1):
            for out, at in ((keep, 2 * j * half), (send, (2 * j + 1) * half)):
                out[i + j, :, :own] = part[at : at + half]
                out[i + j, :, own:] = padding


def activate(own, keep, got, keep_hidden, got_hidden, out):
    width = out.shape[2] // 3
    padding = jnp.zeros((out.shape[1], 3 * width - (width + 2 * own)), BF16)
    for i in range(out.shape[0]):
        gate_sum, up_sum = (
            add(keep[i, :, k * width : (k + 1) * width], got[i, :, k * width : (k + 1) * width])
            for k in range(2)
        )
        grad_hidden = add(keep_hidden[i], got_hidden[i])
        sigmoid_gate = jax.nn.sigmoid(gate_sum)
        out[i, :, :width] = (gate_sum * sigmoid_gate * up_sum).astype(BF16)
        grad_gate_act = grad_hidden * up_sum * sigmoid_gate * (1.0 + gate_sum * (1.0 - sigmoid_gate))
        out[i, :, width : 2 * width] = grad_gate_act.astype(BF16)
        grad_up_act = (grad_hidden * gate_sum * sigmoid_gate).astype(BF16)
        out[i, :, width + own : width + 2 * own] = grad_up_act[:, :own]
        out[i, :, width + 2 * own :] = padding


def output_products(copy, sources, results, hidden, down):
    copies = copy_part(copy, sources[0], sources[1], 0, hidden)
    wait_all(copies + copy_down(copy, *sources[2:], down))
    own, first = down.shape[0], 0
    for out in results:
        rows = out.shape[0]
        out[...] = dot(hidden[pl.ds(first, rows), :own], down[...], 1, 0).astype(BF16)
        first += rows


def input_products(copy, sources, results, acts, pair):
    copies = copy_part(copy, sources[0], sources[1], acts.shape[1] // 2, acts)
    wait_all(copies + copy_pair(copy, *sources[2:], pair))
    both = pair.shape[0]
    count, features = results[0].shape[1] // 2, pair.shape[1] // 2
    for k, out in enumerate(results):
        for side in (0, 1):
            place = pl.ds(pl.multiple_of(side * features + own_place(k, count), count), count)
            part = dot(acts[:, :both], pair[:, place], 1, 0)
            out[:, side * count : (side + 1) * count] = part.astype(BF16)


def pair_gradients(scale, copy, sources, results, tokens, acts):
    copies = copy_tokens(copy, sources[:5], tokens)
    wait_all(copies + copy_part(copy, *sources[5:], acts.shape[1] // 2, acts))
    near, far = results
    groups, both, count = near.shape
    features = groups * count
    for out, first in ((far, features), (near, 0)):
        total = dot(acts[:, :both], tokens[:, pl.ds(first, features)], 0, 0) * scale
        for g in range(groups):
            out[g] = total[:, g * count : (g + 1) * count].astype(BF16)


def down_gradients(scale, copy, sources, results, grads, hidden):
    copies = copy_grads(copy, sources[:5], grads)
    wait_all(copies + copy_part(copy, *sources[5:], 0, hidden))
    near, far = results
    own, features = near.shape
    for out, first in ((far, features), (near, 0)):
        total = dot(hidden[:, :own], grads[:, pl.ds(first, features)], 0, 0)
        out[...] = (total * scale).astype(BF16)


def split_result(*refs):
    *parts, near, far, near_x, far_x = refs
    half, count = near.shape[0], near.shape[1] // 2
    core = core_index()
    for first, arrays in ((0, parts[:4]), (count, parts[4:])):
        for index, left, right in ((core, near, far), (1 - core, near_x, far_x)):
            rows = sum(array[block(index, half)].astype(F32) for array in arrays).astype(BF16)
            left[:, first : first + count] = rows[:, :count]
            right[:, first : first + count] = rows[:, count:]


def join_result(near, near_x, far, far_x, output, grad_input):
    half, count = near.shape[0], near.shape[1] // 2
    for parts, index in (((near, near_x), x_lo_index()), ((far, far_x), 1 - x_lo_index())):
        rows = add(parts[0][...], parts[1][...]).astype(BF16)
        output[block(index, half)] = rows[:, :count]
        grad_input[block(index, half)] = rows[:, count:]


def ring_gather(shift, array):
    half = array.shape[0] // 2
    before, after = shift(array, 1), shift(array, -1)
    return [array, before, shift(before[:half], 1), shift(after[half:], -1), after]


def direct_gather(shift, array):
    return [array, shift(array, 1), shift(array, 2), shift(array, -1)]


def direct_scatter(shift, own, before, opposite, after):
    return [own, shift(before, -1), shift(after, 1), shift(opposite, 2)]


def on_device(tokens, w_gate, w_up, w_down, grad_output):
    tok_rows, tok_columns = tokens.shape
    rows_in, width_hidden = w_gate.shape
    own = width_hidden // 8
    width = -(-own // LANES) * LANES
    features = 8 * rows_in
    loss_scale = 1.0 / math.sqrt(tok_rows * 8)
    rows, columns = tok_rows // 2, 2 * tok_columns

    mine, theirs = local_call(split_rows, [(rows, columns)] * 2, [tokens, grad_output])
    four = [mine, swap_x_lo(theirs), swap_x_hi(mine), swap_x(theirs)]
    t_block, g_block = local_call(arrange_rows, [(2 * rows, columns)] * 2, four)

    (pieces,) = local_call(split_pair, [(8, 2 * own, rows_in)], [w_gate, w_up])
    w_near = lax.all_to_all(after(pieces, *four), "gx", 0, 0, tiled=True)
    d_near, d_far = w_down, swap_x_lo(after(w_down, *four))

    (t_own,) = local_call(
        join_features, [(2 * rows, 2 * features)], direct_gather(shift_y, t_block)
    )
    g_own = jnp.concatenate(direct_gather(shift_z, g_block), axis=0)
    t_own, g_own, w_near, d_far = lax.optimization_barrier((t_own, g_own, w_near, d_far))
    w_far = swap_x_lo(w_near)
    t_all = ring_gather(shift_z, t_own)
    g_all = ring_gather(shift_y, g_own)

    all_tokens, all_features = 8 * rows, 2 * features
    whole = (all_tokens, all_features)
    keep_hidden, send_hidden = assembled_call(
        hidden_products,
        [(4, rows, width)] * 2,
        [*g_all, d_near, d_far],
        [whole, (own, all_features)],
        12,
    )
    got_hidden = swap_core(send_hidden)
    half_features = (all_tokens, features)
    (share,) = assembled_call(
        near_products,
        [(all_tokens, 2 * own)],
        [*t_all, w_near],
        [half_features, (2 * own, features)],
        13,
        dtype=F32,
    )
    keep, send = assembled_call(
        pair_products,
        [(4, rows, 2 * width)] * 2,
        [*t_all[:4], after(t_all[4], got_hidden), w_far, share],
        [half_features, (2 * own, features), ((all_tokens, 2 * own), F32)],
        15,
    )
    (mine,) = local_call(
        functools.partial(activate, own),
        [(4, rows, 3 * width)],
        [keep, swap_core(send), keep_hidden, got_hidden],
    )
    both = [mine, swap_core(mine)]

    near, far = assembled_call(
        functools.partial(pair_gradients, loss_scale),
        [(8, 2 * own, rows_in)] * 2,
        [*t_all, *both],
        [whole, (all_tokens, 2 * width)],
        13,
    )
    both[1] = after(both[1], near)
    output_parts = assembled_call(
        output_products,
        [(size * rows, all_features) for size in (2, 2, 1, 1, 2)],
        [*both, d_near, d_far],
        [(all_tokens, width), (own, all_features)],
        10,
    )
    both[1] = after(both[1], output_parts[2])
    input_parts = assembled_call(
        input_products,
        [(all_tokens, columns)] * 4,
        [*both, w_near, w_far],
        [(all_tokens, 2 * width), (2 * own, all_features)],
        24,
    )
    both[1] = after(both[1], input_parts[2])
    down_near, down_far = assembled_call(
        functools.partial(down_gradients, loss_scale),
        [(own, features)] * 2,
        [*g_all, *both],
        [whole, (all_tokens, width)],
        18,
    )

    grad_pair = add(near, swap_x_lo(far)).astype(BF16)
    down_far = after(down_far, grad_pair)
    total = lax.all_to_all(after(grad_pair, down_near), "gx", 0, 0, tiled=True)
    grad_down = add(down_near, swap_x_lo(down_far)).astype(BF16)

    own, before, low, high, after_it = output_parts
    from_z = shift_z(low, 1), shift_z(high, -1)
    after_it = lax.dynamic_update_slice(
        after_it, add(after_it[:rows], from_z[0]).astype(BF16), (0, 0)
    )
    before = lax.dynamic_update_slice(
        before, add(before[rows:], from_z[1]).astype(BF16), (rows, 0)
    )
    output = own.astype(F32) + shift_z(after_it, 1).astype(F32)
    output = (output + shift_z(before, -1).astype(F32)).astype(BF16)
    own, before, opposite, after_it = input_parts
    from_y = shift_y(before, -1), shift_y(after_it, 1)
    opposite = after(opposite, *from_y, *from_z)
    grad_input = own.astype(F32) + from_y[0].astype(F32) + from_y[1].astype(F32)
    grad_input = (grad_input + shift_y(opposite, 2).astype(F32)).astype(BF16)
    output = after(output, grad_input)
    grad_input = after(grad_input, total)
    parts = [grad_input[2 * k * rows : 2 * (k + 1) * rows] for k in range(4)]
    input_parts = direct_scatter(shift_z, *parts)
    parts = local_call(pick_features, [(2 * rows, columns)] * 4, [output])
    output_parts = direct_scatter(shift_y, *parts)
    grads = local_call(join_blocks, [(rows_in, width_hidden)] * 2, [total])
    output_parts[0], grad_down, *grads = lax.optimization_barrier(
        (output_parts[0], grad_down, *grads)
    )
    near, far, near_x, far_x = local_call(
        split_result, [(rows, columns)] * 4, [*output_parts, *input_parts]
    )
    four = [near, swap_x_hi(near_x), swap_x_lo(far), swap_x(far_x)]
    output, grad_input = local_call(join_result, [tokens.shape] * 2, four)
    return (output, grad_input, *grads, grad_down)


def solution(mesh):
    placed = (
        P("gx", ("gz", "gy")),
        P(("gz", "gx"), "gy"),
        P(("gz", "gx"), "gy"),
        P(("gy", "gx"), "gz"),
        P("gx", ("gz", "gy")),
    )
    return jax.shard_map(
        on_device,
        mesh=mesh,
        in_specs=placed,
        out_specs=(
            P("gx", ("gz", "gy")),
            P("gx", ("gz", "gy")),
            P(("gz", "gx"), "gy"),
            P(("gz", "gx"), "gy"),
            P(("gy", "gx"), "gz"),
        ),
        check_vma=False,
    )
```

```python
import functools
import math

import jax
import jax.numpy as jnp
from jax import lax
from jax.experimental import pallas as pl
from jax.experimental.pallas import tpu as pltpu
from jax.sharding import PartitionSpec as P


BF16 = jnp.bfloat16
F32 = jnp.float32
LANES = 128


def shift_z(array, steps):
    return lax.ppermute(
        array, "gx", [(i, ((i // 2 + steps) % 4) * 2 + i % 2) for i in range(8)]
    )


def shift_y(array, steps):
    return lax.ppermute(array, "gy", [(i, (i + steps) % 4) for i in range(4)])


def swap_x_hi(array):
    return lax.ppermute(array, "gx", [(i, i ^ 1) for i in range(8)])


def swap_x_lo(array):
    return lax.ppermute(array, "gz", [(i, i ^ 2) for i in range(4)])


def swap_x(array):
    return lax.ppermute(array, ("gx", "gz"), [(i, i ^ 6) for i in range(32)])


def swap_core(array):
    return lax.ppermute(array, "gz", [(i, i ^ 1) for i in range(4)])


def add(left_side, right_side):
    return left_side.astype(F32) + right_side.astype(F32)


def dot(left_side, right_side, left_dim, right_dim):
    return lax.dot_general(
        left_side,
        right_side,
        (((left_dim,), (right_dim,)), ((), ())),
        preferred_element_type=F32,
    )


class Operand:
    def __init__(self, source, held, semaphore):
        self.copy = pltpu.make_async_copy(source, held, semaphore)
        self.copy.start()
        self.held = held
        self.shape = held.shape

    def ready(self):
        if self.copy is not None:
            self.copy.wait()
            self.copy = None
        return self.held

    def __getitem__(self, index):
        return self.ready()[index]


def local_call(kernel, out_shapes, operands, scratch_shapes=(), vmem=40):
    count, outs = len(operands), len(out_shapes)

    def body(*refs):
        sources, refs = refs[:count], refs[count:]
        results, refs = refs[:outs], refs[outs:]
        held, semaphores, scratch = refs[:count], refs[count], refs[count + 1 :]
        inputs = [
            Operand(source, place, semaphores.at[i])
            for i, (source, place) in enumerate(zip(sources, held))
        ]
        kernel(*inputs, *results, *scratch)
        for operand in inputs:
            operand.ready()

    return list(
        pl.pallas_call(
            body,
            out_shape=[jax.ShapeDtypeStruct(shape, BF16) for shape in out_shapes],
            in_specs=[pl.BlockSpec(memory_space=pl.ANY)] * count,
            out_specs=[pl.BlockSpec(memory_space=pltpu.VMEM)] * outs,
            scratch_shapes=[
                *(pltpu.VMEM(array.shape, BF16) for array in operands),
                pltpu.SemaphoreType.DMA((count,)),
                *scratch_shapes,
            ],
            compiler_params=pltpu.CompilerParams(vmem_limit_bytes=vmem * 2**20),
        )(*operands)
    )


def assembled_call(kernel, out_shapes, operands, buffers, copies, vmem=40, dtype=BF16):
    count, outs = len(operands), len(out_shapes)
    buffers = [buffer if len(buffer) == 2 and isinstance(buffer[0], tuple) else (buffer, BF16) for buffer in buffers]

    def body(*refs):
        sources, refs = refs[:count], refs[count:]
        results, (*held, semaphores) = refs[:outs], refs[outs:]
        started = []

        def copy(source, target):
            started.append(pltpu.make_async_copy(source, target, semaphores.at[len(started)]))
            started[-1].start()
            return started[-1]

        kernel(copy, sources, results, *held)

    return list(
        pl.pallas_call(
            body,
            out_shape=[jax.ShapeDtypeStruct(shape, dtype) for shape in out_shapes],
            in_specs=[pl.BlockSpec(memory_space=pl.ANY)] * count,
            out_specs=[pl.BlockSpec(memory_space=pltpu.VMEM)] * outs,
            scratch_shapes=[
                *(pltpu.VMEM(*buffer) for buffer in buffers),
                pltpu.SemaphoreType.DMA((copies,)),
            ],
            compiler_params=pltpu.CompilerParams(vmem_limit_bytes=vmem * 2**20),
        )(*operands)
    )


def wait_all(copies):
    for copy in copies:
        copy.wait()


def after(array, *earlier):
    return lax.optimization_barrier((array, *earlier))[0]


def core_index():
    return lax.rem(lax.axis_index("gz"), 2)


def x_lo_index():
    return lax.div(lax.axis_index("gz"), 2)


def block(index, count):
    return pl.ds(pl.multiple_of(index * count, count), count)


def feature_block(k, count):
    return block(lax.rem(lax.axis_index("gy") + (4 - k), 4), count)


def split_rows(tokens, grads, mine, theirs):
    half, count = mine.shape[0], tokens.shape[1]
    for out, index in ((mine, x_lo_index()), (theirs, 1 - x_lo_index())):
        out[:, :count] = tokens[block(index, half)]
        out[:, count:] = grads[block(index, half)]


def arrange_rows(near, far, near_x, far_x, tokens, grads):
    half, count = near.shape[0], near.shape[1] // 2
    core = core_index()
    for index, left, right in ((core, near, far), (1 - core, near_x, far_x)):
        tokens[block(index, half), :count] = left[:, :count]
        tokens[block(index, half), count:] = right[:, :count]
        grads[block(index, half), :count] = left[:, count:]
        grads[block(index, half), count:] = right[:, count:]


def split_pair(w_gate, w_up, out):
    groups, own = out.shape[0], out.shape[1] // 2
    for first, array in ((0, w_gate), (own, w_up)):
        for g in range(groups):
            out[g, first : first + own] = array[:, g * own : (g + 1) * own].T


def join_blocks(pieces, gate, up):
    groups, both, _ = pieces.shape
    own = both // 2
    for g in range(groups):
        gate[:, g * own : (g + 1) * own] = pieces[g, :own].T
        up[:, g * own : (g + 1) * own] = pieces[g, own:].T


def join_features(*refs):
    *blocks, out = refs
    count, features = blocks[0].shape[1] // 2, out.shape[1] // 2
    for k, part in enumerate(blocks):
        place = lax.rem(lax.axis_index("gy") + (4 - k), 4) * count
        out[:, pl.ds(pl.multiple_of(place, count), count)] = part[:, :count]
        out[:, pl.ds(pl.multiple_of(features + place, count), count)] = part[:, count:]


def pick_features(whole, *outs):
    count, features = outs[0].shape[1] // 2, whole.shape[1] // 2
    for k, out in enumerate(outs):
        place = lax.rem(lax.axis_index("gy") + (4 - k), 4) * count
        out[:, :count] = whole[:, pl.ds(pl.multiple_of(place, count), count)]
        out[:, count:] = whole[:, pl.ds(pl.multiple_of(features + place, count), count)]


def own_place(k, count):
    return lax.rem(lax.axis_index("gy") + (4 - k), 4) * count


def copy_tokens(copy, refs, held):
    copies, first = [], 0
    for ref in refs:
        copies.append(copy(ref, held.at[pl.ds(first, ref.shape[0])]))
        first += ref.shape[0]
    return copies


def copy_grads(copy, refs, held):
    copies = []
    count, features = refs[0].shape[1] // 2, held.shape[1] // 2
    for ref, k, first in zip(refs, (0, 1, 2, 2, 3), (0, 0, 0, refs[2].shape[0], 0)):
        for side in (0, 1):
            place = side * features + own_place(k, count)
            target = held.at[
                pl.ds(first, ref.shape[0]), pl.ds(pl.multiple_of(place, count), count)
            ]
            copies.append(copy(ref.at[:, pl.ds(side * count, count)], target))
    return copies


def copy_blocks(copy, ref, held):
    groups, _, count = ref.shape
    return [copy(ref.at[g], held.at[:, pl.ds(g * count, count)]) for g in range(groups)]


def copy_pair(copy, near, far, held):
    features = held.shape[1] // 2
    copies = copy_blocks(copy, near, held.at[:, pl.ds(0, features)])
    return copies + copy_blocks(copy, far, held.at[:, pl.ds(features, features)])


def copy_down(copy, near, far, held):
    features = near.shape[1]
    return [
        copy(ref, held.at[:, pl.ds(side * features, features)])
        for side, ref in enumerate((near, far))
    ]


def copy_part(copy, mine, other, first, held):
    rows, width = mine.shape[1], held.shape[1]
    return [
        copy(
            ref.at[i, :, pl.ds(first, width)], held.at[pl.ds((2 * i + side) * rows, rows)]
        )
        for i in range(mine.shape[0])
        for side, ref in enumerate((mine, other))
    ]


def near_products(copy, sources, results, tokens, pair):
    features = tokens.shape[1]
    copies = copy_blocks(copy, sources[3], pair)
    copies += copy_tokens(copy, [ref.at[:, pl.ds(0, features)] for ref in sources[:3]], tokens)
    wait_all(copies)
    results[0][...] = dot(tokens[...], pair[...], 1, 1)


def pair_products(copy, sources, results, tokens, pair, share, opposite, near):
    keep, send = results
    half, width = keep.shape[1], keep.shape[2] // 2
    own = pair.shape[0] // 2
    features = tokens.shape[1]
    copies = copy_blocks(copy, sources[5], pair)
    chunks = copy_tokens(
        copy, [ref.at[:, pl.ds(features, features)] for ref in sources[:5]], tokens
    )
    chunks.append(copy(sources[6], share))
    later = copy_blocks(copy, sources[7], near)
    later += copy_tokens(
        copy, [ref.at[:, pl.ds(0, features)] for ref in sources[2:4]], opposite
    )
    wait_all(copies + chunks)
    padding = jnp.zeros((half, width - own), BF16)
    for i in (0, 2):
        part = dot(tokens[pl.ds(2 * i * half, 4 * half)], pair[...], 1, 1)
        if i == 0:
            part = part + share[pl.ds(0, 4 * half)]
        else:
            wait_all(later)
            first = part[: 2 * half] + dot(opposite[...], near[...], 1, 1)
            part = jnp.concatenate([first, part[2 * half :] + share[pl.ds(4 * half, 2 * half)]])
        part = part.astype(BF16)
        for j in (0, 1):
            for out, at in ((keep, 2 * j * half), (send, (2 * j + 1) * half)):
                piece = part[at : at + half]
                for k in (0, 1):
                    out[i + j, :, k * width : k * width + own] = piece[:, k * own : (k + 1) * own]
                    out[i + j, :, k * width + own : (k + 1) * width] = padding


def copy_down_blocks(copy, near, far, blocks, held):
    count = held.shape[1] // (2 * len(blocks))
    return [
        copy(
            ref.at[:, feature_block(k, count)],
            held.at[:, pl.ds((2 * i + side) * count, count)],
        )
        for i, k in enumerate(blocks)
        for side, ref in enumerate((near, far))
    ]


def early_hidden_products(copy, sources, results, grads, down):
    columns = sources[0].shape[1]
    copies = copy_down_blocks(copy, *sources[3:], (0, 1, 3), down)
    copies += [
        copy(ref, grads.at[:, pl.ds(i * columns, columns)]) for i, ref in enumerate(sources[:3])
    ]
    wait_all(copies)
    results[0][...] = dot(grads[...], down[...], 1, 1)


def hidden_products(copy, sources, results, grads, down, share):
    keep, send = results
    half, width = keep.shape[1:]
    own = down.shape[0]
    copies = copy_down_blocks(copy, *sources[2:4], (2,), down)
    copies += copy_tokens(copy, sources[:2], grads)
    wait_all(copies + [copy(sources[4], share)])
    padding = jnp.zeros((half, width - own), BF16)
    for i in (0, 2):
        here = pl.ds(2 * i * half, 4 * half)
        part = (dot(grads[here], down[...], 1, 1) + share[here]).astype(BF16)
        for j in (0, 1):
            for out, at in ((keep, 2 * j * half), (send, (2 * j + 1) * half)):
                out[i + j, :, :own] = part[at : at + half]
                out[i + j, :, own:] = padding


def activate(own, keep, got, keep_hidden, got_hidden, out):
    width = out.shape[2] // 3
    padding = jnp.zeros((out.shape[1], 3 * width - (width + 2 * own)), BF16)
    for i in range(out.shape[0]):
        gate_sum, up_sum = (
            add(keep[i, :, k * width : (k + 1) * width], got[i, :, k * width : (k + 1) * width])
            for k in range(2)
        )
        grad_hidden = add(keep_hidden[i], got_hidden[i])
        sigmoid_gate = jax.nn.sigmoid(gate_sum)
        out[i, :, :width] = (gate_sum * sigmoid_gate * up_sum).astype(BF16)
        grad_gate_act = grad_hidden * up_sum * sigmoid_gate * (1.0 + gate_sum * (1.0 - sigmoid_gate))
        out[i, :, width : 2 * width] = grad_gate_act.astype(BF16)
        grad_up_act = (grad_hidden * gate_sum * sigmoid_gate).astype(BF16)
        out[i, :, width + own : width + 2 * own] = grad_up_act[:, :own]
        out[i, :, width + 2 * own :] = padding


def output_products(copy, sources, results, hidden, down):
    copies = copy_part(copy, sources[0], sources[1], 0, hidden)
    wait_all(copies + copy_down(copy, *sources[2:], down))
    own, first = down.shape[0], 0
    for out in results:
        rows = out.shape[0]
        out[...] = dot(hidden[pl.ds(first, rows), :own], down[...], 1, 0).astype(BF16)
        first += rows


def input_products(copy, sources, results, acts, pair):
    copies = copy_part(copy, sources[0], sources[1], acts.shape[1] // 2, acts)
    wait_all(copies + copy_pair(copy, *sources[2:], pair))
    both = pair.shape[0]
    count, features = results[0].shape[1] // 2, pair.shape[1] // 2
    for k, out in enumerate(results):
        for side in (0, 1):
            place = pl.ds(pl.multiple_of(side * features + own_place(k, count), count), count)
            part = dot(acts[:, :both], pair[:, place], 1, 0)
            out[:, side * count : (side + 1) * count] = part.astype(BF16)


def pair_gradients(scale, side, copy, sources, results, tokens, acts):
    groups, both, count = results[0].shape
    features = groups * count
    columns = [ref.at[:, pl.ds(side * features, features)] for ref in sources[:5]]
    copies = copy_tokens(copy, columns, tokens)
    wait_all(copies + copy_part(copy, *sources[5:], acts.shape[1] // 2, acts))
    total = dot(acts[:, :both], tokens[...], 0, 0) * scale
    for g in range(groups):
        results[0][g] = total[:, g * count : (g + 1) * count].astype(BF16)


def down_gradients(scale, copy, sources, results, grads, hidden):
    copies = copy_grads(copy, sources[:5], grads)
    wait_all(copies + copy_part(copy, *sources[5:], 0, hidden))
    near, far = results
    own, features = near.shape
    for out, first in ((far, features), (near, 0)):
        total = dot(hidden[:, :own], grads[:, pl.ds(first, features)], 0, 0)
        out[...] = (total * scale).astype(BF16)


def split_result(*refs):
    *parts, near, far, near_x, far_x = refs
    half, count = near.shape[0], near.shape[1] // 2
    core = core_index()
    for first, arrays in ((0, parts[:4]), (count, parts[4:])):
        for index, left, right in ((core, near, far), (1 - core, near_x, far_x)):
            rows = sum(array[block(index, half)].astype(F32) for array in arrays).astype(BF16)
            left[:, first : first + count] = rows[:, :count]
            right[:, first : first + count] = rows[:, count:]


def join_result(near, near_x, far, far_x, output, grad_input):
    half, count = near.shape[0], near.shape[1] // 2
    for parts, index in (((near, near_x), x_lo_index()), ((far, far_x), 1 - x_lo_index())):
        rows = add(parts[0][...], parts[1][...]).astype(BF16)
        output[block(index, half)] = rows[:, :count]
        grad_input[block(index, half)] = rows[:, count:]


def ring_gather(shift, array):
    half = array.shape[0] // 2
    before, after = shift(array, 1), shift(array, -1)
    return [array, before, shift(before[:half], 1), shift(after[half:], -1), after]


def direct_gather(shift, array):
    return [array, shift(array, 1), shift(array, 2), shift(array, -1)]


def direct_scatter(shift, own, before, opposite, after):
    return [own, shift(before, -1), shift(after, 1), shift(opposite, 2)]


def on_device(tokens, w_gate, w_up, w_down, grad_output):
    tok_rows, tok_columns = tokens.shape
    rows_in, width_hidden = w_gate.shape
    own = width_hidden // 8
    width = -(-own // LANES) * LANES
    features = 8 * rows_in
    loss_scale = 1.0 / math.sqrt(tok_rows * 8)
    rows, columns = tok_rows // 2, 2 * tok_columns

    mine, theirs = local_call(split_rows, [(rows, columns)] * 2, [tokens, grad_output])
    four = [mine, swap_x_lo(theirs), swap_x_hi(mine), swap_x(theirs)]
    t_block, g_block = local_call(arrange_rows, [(2 * rows, columns)] * 2, four)

    (pieces,) = local_call(split_pair, [(8, 2 * own, rows_in)], [w_gate, w_up])
    w_near = lax.all_to_all(after(pieces, *four), "gx", 0, 0, tiled=True)
    d_near, d_far = w_down, swap_x_lo(after(w_down, *four))

    (t_own,) = local_call(
        join_features, [(2 * rows, 2 * features)], direct_gather(shift_y, t_block)
    )
    g_own = jnp.concatenate(direct_gather(shift_z, g_block), axis=0)
    t_own, g_own, w_near, d_far = lax.optimization_barrier((t_own, g_own, w_near, d_far))
    w_far = swap_x_lo(w_near)
    t_all = ring_gather(shift_z, t_own)
    g_all = ring_gather(shift_y, g_own)

    all_tokens, all_features = 8 * rows, 2 * features
    whole = (all_tokens, all_features)
    (share,) = assembled_call(
        near_products,
        [(6 * rows, 2 * own)],
        [t_all[0], t_all[1], t_all[4], w_near],
        [(6 * rows, features), (2 * own, features)],
        11,
        dtype=F32,
    )
    half_features = (all_tokens, features)
    (early,) = assembled_call(
        early_hidden_products,
        [(all_tokens, own)],
        [g_all[0], g_all[1], g_all[4], d_near, d_far],
        [(all_tokens, 3 * columns), (own, 3 * columns)],
        9,
        dtype=F32,
    )
    keep_hidden, send_hidden = assembled_call(
        hidden_products,
        [(4, rows, width)] * 2,
        [g_all[2], after(g_all[3], share), d_near, d_far, early],
        [(all_tokens, columns), (own, columns), ((all_tokens, own), F32)],
        5,
    )
    got_hidden = swap_core(send_hidden)
    weights = (2 * own, features)
    keep, send = assembled_call(
        pair_products,
        [(4, rows, 2 * width)] * 2,
        [*t_all[:4], after(t_all[4], keep_hidden), w_far, share, w_near],
        [half_features, weights, ((6 * rows, 2 * own), F32), (2 * rows, features), weights],
        24,
    )
    (mine,) = local_call(
        functools.partial(activate, own),
        [(4, rows, 3 * width)],
        [keep, swap_core(send), keep_hidden, got_hidden],
    )
    both = [mine, swap_core(mine)]

    def pair_gradient(side):
        return assembled_call(
            functools.partial(pair_gradients, loss_scale, side),
            [(8, 2 * own, rows_in)],
            [*t_all, *both],
            [half_features, (all_tokens, 2 * width)],
            13,
        )[0]

    far = pair_gradient(1)
    both[1] = after(both[1], far)
    output_parts = assembled_call(
        output_products,
        [(size * rows, all_features) for size in (2, 2, 1, 1, 2)],
        [*both, d_near, d_far],
        [(all_tokens, width), (own, all_features)],
        10,
    )
    both[1] = after(both[1], output_parts[2])
    input_parts = assembled_call(
        input_products,
        [(all_tokens, columns)] * 4,
        [*both, w_near, w_far],
        [(all_tokens, 2 * width), (2 * own, all_features)],
        24,
    )
    both[1] = after(both[1], input_parts[2])
    near = pair_gradient(0)
    down_near, down_far = assembled_call(
        functools.partial(down_gradients, loss_scale),
        [(own, features)] * 2,
        [*g_all, *both],
        [whole, (all_tokens, width)],
        18,
    )

    grad_pair = add(near, swap_x_lo(far)).astype(BF16)
    down_far = after(down_far, grad_pair)
    total = lax.all_to_all(after(grad_pair, down_near), "gx", 0, 0, tiled=True)
    grad_down = add(down_near, swap_x_lo(down_far)).astype(BF16)

    own, before, low, high, after_it = output_parts
    from_z = shift_z(low, 1), shift_z(high, -1)
    after_it = lax.dynamic_update_slice(
        after_it, add(after_it[:rows], from_z[0]).astype(BF16), (0, 0)
    )
    before = lax.dynamic_update_slice(
        before, add(before[rows:], from_z[1]).astype(BF16), (rows, 0)
    )
    output = own.astype(F32) + shift_z(after_it, 1).astype(F32)
    output = (output + shift_z(before, -1).astype(F32)).astype(BF16)
    own, before, opposite, after_it = input_parts
    from_y = shift_y(before, -1), shift_y(after_it, 1)
    opposite = after(opposite, *from_y, *from_z)
    grad_input = own.astype(F32) + from_y[0].astype(F32) + from_y[1].astype(F32)
    grad_input = (grad_input + shift_y(opposite, 2).astype(F32)).astype(BF16)
    output = after(output, grad_input)
    grad_input = after(grad_input, total)
    parts = [grad_input[2 * k * rows : 2 * (k + 1) * rows] for k in range(4)]
    input_parts = direct_scatter(shift_z, *parts)
    parts = local_call(pick_features, [(2 * rows, columns)] * 4, [output])
    output_parts = direct_scatter(shift_y, *parts)
    grads = local_call(join_blocks, [(rows_in, width_hidden)] * 2, [total])
    output_parts[0], grad_down, *grads = lax.optimization_barrier(
        (output_parts[0], grad_down, *grads)
    )
    near, far, near_x, far_x = local_call(
        split_result, [(rows, columns)] * 4, [*output_parts, *input_parts]
    )
    four = [near, swap_x_hi(near_x), swap_x_lo(far), swap_x(far_x)]
    output, grad_input = local_call(join_result, [tokens.shape] * 2, four)
    return (output, grad_input, *grads, grad_down)


def solution(mesh):
    placed = (
        P("gx", ("gz", "gy")),
        P(("gz", "gx"), "gy"),
        P(("gz", "gx"), "gy"),
        P(("gy", "gx"), "gz"),
        P("gx", ("gz", "gy")),
    )
    return jax.shard_map(
        on_device,
        mesh=mesh,
        in_specs=placed,
        out_specs=(
            P("gx", ("gz", "gy")),
            P("gx", ("gz", "gy")),
            P(("gz", "gx"), "gy"),
            P(("gz", "gx"), "gy"),
            P(("gy", "gx"), "gz"),
        ),
        check_vma=False,
    )
```

```python
import functools
import math

import jax
import jax.numpy as jnp
from jax import lax
from jax.experimental import pallas as pl
from jax.experimental.pallas import tpu as pltpu
from jax.sharding import PartitionSpec as P


BF16 = jnp.bfloat16
F32 = jnp.float32
LANES = 128


def shift_z(array, steps):
    return lax.ppermute(
        array, "gx", [(i, ((i // 2 + steps) % 4) * 2 + i % 2) for i in range(8)]
    )


def shift_y(array, steps):
    return lax.ppermute(array, "gy", [(i, (i + steps) % 4) for i in range(4)])


def swap_x_hi(array):
    return lax.ppermute(array, "gx", [(i, i ^ 1) for i in range(8)])


def swap_x_lo(array):
    return lax.ppermute(array, "gz", [(i, i ^ 2) for i in range(4)])


def swap_x(array):
    return lax.ppermute(array, ("gx", "gz"), [(i, i ^ 6) for i in range(32)])


def swap_core(array):
    return lax.ppermute(array, "gz", [(i, i ^ 1) for i in range(4)])


def add(left_side, right_side):
    return left_side.astype(F32) + right_side.astype(F32)


def dot(left_side, right_side, left_dim, right_dim):
    return lax.dot_general(
        left_side,
        right_side,
        (((left_dim,), (right_dim,)), ((), ())),
        preferred_element_type=F32,
    )


class Operand:
    def __init__(self, source, held, semaphore):
        self.copy = pltpu.make_async_copy(source, held, semaphore)
        self.copy.start()
        self.held = held
        self.shape = held.shape

    def ready(self):
        if self.copy is not None:
            self.copy.wait()
            self.copy = None
        return self.held

    def __getitem__(self, index):
        return self.ready()[index]


def local_call(kernel, out_shapes, operands, scratch_shapes=(), vmem=40):
    count, outs = len(operands), len(out_shapes)

    def body(*refs):
        sources, refs = refs[:count], refs[count:]
        results, refs = refs[:outs], refs[outs:]
        held, semaphores, scratch = refs[:count], refs[count], refs[count + 1 :]
        inputs = [
            Operand(source, place, semaphores.at[i])
            for i, (source, place) in enumerate(zip(sources, held))
        ]
        kernel(*inputs, *results, *scratch)
        for operand in inputs:
            operand.ready()

    return list(
        pl.pallas_call(
            body,
            out_shape=[jax.ShapeDtypeStruct(shape, BF16) for shape in out_shapes],
            in_specs=[pl.BlockSpec(memory_space=pl.ANY)] * count,
            out_specs=[pl.BlockSpec(memory_space=pltpu.VMEM)] * outs,
            scratch_shapes=[
                *(pltpu.VMEM(array.shape, BF16) for array in operands),
                pltpu.SemaphoreType.DMA((count,)),
                *scratch_shapes,
            ],
            compiler_params=pltpu.CompilerParams(vmem_limit_bytes=vmem * 2**20),
        )(*operands)
    )


def assembled_call(kernel, out_shapes, operands, buffers, copies, vmem=40, dtype=BF16):
    count, outs = len(operands), len(out_shapes)
    buffers = [buffer if len(buffer) == 2 and isinstance(buffer[0], tuple) else (buffer, BF16) for buffer in buffers]

    def body(*refs):
        sources, refs = refs[:count], refs[count:]
        results, (*held, semaphores) = refs[:outs], refs[outs:]
        started = []

        def copy(source, target):
            started.append(pltpu.make_async_copy(source, target, semaphores.at[len(started)]))
            started[-1].start()
            return started[-1]

        kernel(copy, sources, results, *held)

    return list(
        pl.pallas_call(
            body,
            out_shape=[jax.ShapeDtypeStruct(shape, dtype) for shape in out_shapes],
            in_specs=[pl.BlockSpec(memory_space=pl.ANY)] * count,
            out_specs=[pl.BlockSpec(memory_space=pltpu.VMEM)] * outs,
            scratch_shapes=[
                *(pltpu.VMEM(*buffer) for buffer in buffers),
                pltpu.SemaphoreType.DMA((copies,)),
            ],
            compiler_params=pltpu.CompilerParams(vmem_limit_bytes=vmem * 2**20),
        )(*operands)
    )


def wait_all(copies):
    for copy in copies:
        copy.wait()


def after(array, *earlier):
    return lax.optimization_barrier((array, *earlier))[0]


def core_index():
    return lax.rem(lax.axis_index("gz"), 2)


def x_lo_index():
    return lax.div(lax.axis_index("gz"), 2)


def block(index, count):
    return pl.ds(pl.multiple_of(index * count, count), count)


def feature_block(k, count):
    return block(lax.rem(lax.axis_index("gy") + (4 - k), 4), count)


def split_rows(tokens, grads, mine, theirs):
    half, count = mine.shape[0], tokens.shape[1]
    for out, index in ((mine, x_lo_index()), (theirs, 1 - x_lo_index())):
        out[:, :count] = tokens[block(index, half)]
        out[:, count:] = grads[block(index, half)]


def arrange_rows(near, far, near_x, far_x, tokens, grads):
    half, count = near.shape[0], near.shape[1] // 2
    core = core_index()
    for index, left, right in ((core, near, far), (1 - core, near_x, far_x)):
        tokens[block(index, half), :count] = left[:, :count]
        tokens[block(index, half), count:] = right[:, :count]
        grads[block(index, half), :count] = left[:, count:]
        grads[block(index, half), count:] = right[:, count:]


def split_pair(w_gate, w_up, out):
    groups, own = out.shape[0], out.shape[1] // 2
    for first, array in ((0, w_gate), (own, w_up)):
        for g in range(groups):
            out[g, first : first + own] = array[:, g * own : (g + 1) * own].T


def join_blocks(pieces, gate, up):
    groups, both, _ = pieces.shape
    own = both // 2
    for g in range(groups):
        gate[:, g * own : (g + 1) * own] = pieces[g, :own].T
        up[:, g * own : (g + 1) * own] = pieces[g, own:].T


def join_features(*refs):
    *blocks, out = refs
    count, features = blocks[0].shape[1] // 2, out.shape[1] // 2
    for k, part in enumerate(blocks):
        place = lax.rem(lax.axis_index("gy") + (4 - k), 4) * count
        out[:, pl.ds(pl.multiple_of(place, count), count)] = part[:, :count]
        out[:, pl.ds(pl.multiple_of(features + place, count), count)] = part[:, count:]


def pick_features(whole, *outs):
    count, features = outs[0].shape[1] // 2, whole.shape[1] // 2
    for k, out in enumerate(outs):
        place = lax.rem(lax.axis_index("gy") + (4 - k), 4) * count
        out[:, :count] = whole[:, pl.ds(pl.multiple_of(place, count), count)]
        out[:, count:] = whole[:, pl.ds(pl.multiple_of(features + place, count), count)]


def own_place(k, count):
    return lax.rem(lax.axis_index("gy") + (4 - k), 4) * count


def copy_tokens(copy, refs, held):
    copies, first = [], 0
    for ref in refs:
        copies.append(copy(ref, held.at[pl.ds(first, ref.shape[0])]))
        first += ref.shape[0]
    return copies


def copy_grads(copy, refs, held):
    copies = []
    count, features = refs[0].shape[1] // 2, held.shape[1] // 2
    for ref, k, first in zip(refs, (0, 1, 2, 2, 3), (0, 0, 0, refs[2].shape[0], 0)):
        for side in (0, 1):
            place = side * features + own_place(k, count)
            target = held.at[
                pl.ds(first, ref.shape[0]), pl.ds(pl.multiple_of(place, count), count)
            ]
            copies.append(copy(ref.at[:, pl.ds(side * count, count)], target))
    return copies


def copy_blocks(copy, ref, held):
    groups, _, count = ref.shape
    return [copy(ref.at[g], held.at[:, pl.ds(g * count, count)]) for g in range(groups)]


def copy_pair(copy, near, far, held):
    features = held.shape[1] // 2
    copies = copy_blocks(copy, near, held.at[:, pl.ds(0, features)])
    return copies + copy_blocks(copy, far, held.at[:, pl.ds(features, features)])


def copy_down(copy, near, far, held):
    features = near.shape[1]
    return [
        copy(ref, held.at[:, pl.ds(side * features, features)])
        for side, ref in enumerate((near, far))
    ]


def copy_part(copy, mine, other, first, held):
    rows, width = mine.shape[1], held.shape[1]
    return [
        copy(
            ref.at[i, :, pl.ds(first, width)], held.at[pl.ds((2 * i + side) * rows, rows)]
        )
        for i in range(mine.shape[0])
        for side, ref in enumerate((mine, other))
    ]


def near_products(copy, sources, results, tokens, pair):
    features = tokens.shape[1]
    copies = copy_blocks(copy, sources[3], pair)
    copies += copy_tokens(copy, [ref.at[:, pl.ds(0, features)] for ref in sources[:3]], tokens)
    wait_all(copies)
    results[0][...] = dot(tokens[...], pair[...], 1, 1)


def pair_products(copy, sources, results, tokens, pair, share, opposite, near):
    keep, send = results
    half, width = keep.shape[1], keep.shape[2] // 2
    own = pair.shape[0] // 2
    features = tokens.shape[1]
    copies = copy_blocks(copy, sources[5], pair)
    chunks = copy_tokens(
        copy, [ref.at[:, pl.ds(features, features)] for ref in sources[:5]], tokens
    )
    chunks.append(copy(sources[6], share))
    later = copy_blocks(copy, sources[7], near)
    later += copy_tokens(
        copy, [ref.at[:, pl.ds(0, features)] for ref in sources[2:4]], opposite
    )
    wait_all(copies + chunks)
    padding = jnp.zeros((half, width - own), BF16)
    for i in (0, 2):
        part = dot(tokens[pl.ds(2 * i * half, 4 * half)], pair[...], 1, 1)
        if i == 0:
            part = part + share[pl.ds(0, 4 * half)]
        else:
            wait_all(later)
            first = part[: 2 * half] + dot(opposite[...], near[...], 1, 1)
            part = jnp.concatenate([first, part[2 * half :] + share[pl.ds(4 * half, 2 * half)]])
        part = part.astype(BF16)
        for j in (0, 1):
            for out, at in ((keep, 2 * j * half), (send, (2 * j + 1) * half)):
                piece = part[at : at + half]
                for k in (0, 1):
                    out[i + j, :, k * width : k * width + own] = piece[:, k * own : (k + 1) * own]
                    out[i + j, :, k * width + own : (k + 1) * width] = padding


def copy_down_blocks(copy, near, far, blocks, held):
    count = held.shape[1] // (2 * len(blocks))
    return [
        copy(
            ref.at[:, feature_block(k, count)],
            held.at[:, pl.ds((2 * i + side) * count, count)],
        )
        for i, k in enumerate(blocks)
        for side, ref in enumerate((near, far))
    ]


def early_hidden_products(copy, sources, results, grads, down):
    columns = sources[0].shape[1]
    copies = copy_down_blocks(copy, *sources[3:], (0, 1, 3), down)
    copies += [
        copy(ref, grads.at[:, pl.ds(i * columns, columns)]) for i, ref in enumerate(sources[:3])
    ]
    wait_all(copies)
    results[0][...] = dot(grads[...], down[...], 1, 1)


def hidden_products(copy, sources, results, grads, down, share):
    keep, send = results
    half, width = keep.shape[1:]
    own = down.shape[0]
    copies = copy_down_blocks(copy, *sources[2:4], (2,), down)
    copies += copy_tokens(copy, sources[:2], grads)
    wait_all(copies + [copy(sources[4], share)])
    padding = jnp.zeros((half, width - own), BF16)
    for i in (0, 2):
        here = pl.ds(2 * i * half, 4 * half)
        part = (dot(grads[here], down[...], 1, 1) + share[here]).astype(BF16)
        for j in (0, 1):
            for out, at in ((keep, 2 * j * half), (send, (2 * j + 1) * half)):
                out[i + j, :, :own] = part[at : at + half]
                out[i + j, :, own:] = padding


def activate(own, keep, got, keep_hidden, got_hidden, out):
    width = out.shape[2] // 3
    padding = jnp.zeros((out.shape[1], 3 * width - (width + 2 * own)), BF16)
    for i in range(out.shape[0]):
        gate_sum, up_sum = (
            add(keep[i, :, k * width : (k + 1) * width], got[i, :, k * width : (k + 1) * width])
            for k in range(2)
        )
        grad_hidden = add(keep_hidden[i], got_hidden[i])
        sigmoid_gate = jax.nn.sigmoid(gate_sum)
        out[i, :, :width] = (gate_sum * sigmoid_gate * up_sum).astype(BF16)
        grad_gate_act = grad_hidden * up_sum * sigmoid_gate * (1.0 + gate_sum * (1.0 - sigmoid_gate))
        out[i, :, width : 2 * width] = grad_gate_act.astype(BF16)
        grad_up_act = (grad_hidden * gate_sum * sigmoid_gate).astype(BF16)
        out[i, :, width + own : width + 2 * own] = grad_up_act[:, :own]
        out[i, :, width + 2 * own :] = padding


def output_products(copy, sources, results, hidden, down):
    copies = copy_part(copy, sources[0], sources[1], 0, hidden)
    wait_all(copies + copy_down(copy, *sources[2:], down))
    own, first = down.shape[0], 0
    for out in results:
        rows = out.shape[0]
        out[...] = dot(hidden[pl.ds(first, rows), :own], down[...], 1, 0).astype(BF16)
        first += rows


def input_products(copy, sources, results, acts, pair):
    copies = copy_part(copy, sources[0], sources[1], acts.shape[1] // 2, acts)
    wait_all(copies + copy_pair(copy, *sources[2:], pair))
    both = pair.shape[0]
    count, features = results[0].shape[1] // 2, pair.shape[1] // 2
    for k, out in enumerate(results):
        for side in (0, 1):
            place = pl.ds(pl.multiple_of(side * features + own_place(k, count), count), count)
            part = dot(acts[:, :both], pair[:, place], 1, 0)
            out[:, side * count : (side + 1) * count] = part.astype(BF16)


def pair_gradients(scale, side, copy, sources, results, tokens, acts):
    groups, both, count = results[0].shape
    features = groups * count
    columns = [ref.at[:, pl.ds(side * features, features)] for ref in sources[:5]]
    copies = copy_tokens(copy, columns, tokens)
    wait_all(copies + copy_part(copy, *sources[5:], acts.shape[1] // 2, acts))
    total = dot(acts[:, :both], tokens[...], 0, 0) * scale
    for g in range(groups):
        results[0][g] = total[:, g * count : (g + 1) * count].astype(BF16)


def down_gradients(scale, copy, sources, results, grads, hidden):
    copies = copy_grads(copy, sources[:5], grads)
    wait_all(copies + copy_part(copy, *sources[5:], 0, hidden))
    near, far = results
    own, features = near.shape
    for out, first in ((far, features), (near, 0)):
        total = dot(hidden[:, :own], grads[:, pl.ds(first, features)], 0, 0)
        out[...] = (total * scale).astype(BF16)


def split_result(*refs):
    *parts, near, far, near_x, far_x = refs
    half, count = near.shape[0], near.shape[1] // 2
    core = core_index()
    for first, arrays in ((0, parts[:4]), (count, parts[4:])):
        for index, left, right in ((core, near, far), (1 - core, near_x, far_x)):
            rows = sum(array[block(index, half)].astype(F32) for array in arrays).astype(BF16)
            left[:, first : first + count] = rows[:, :count]
            right[:, first : first + count] = rows[:, count:]


def join_result(near, near_x, far, far_x, output, grad_input):
    half, count = near.shape[0], near.shape[1] // 2
    for parts, index in (((near, near_x), x_lo_index()), ((far, far_x), 1 - x_lo_index())):
        rows = add(parts[0][...], parts[1][...]).astype(BF16)
        output[block(index, half)] = rows[:, :count]
        grad_input[block(index, half)] = rows[:, count:]


def ring_gather(shift, array):
    half = array.shape[0] // 2
    before, after = shift(array, 1), shift(array, -1)
    return [array, before, shift(before[:half], 1), shift(after[half:], -1), after]


def direct_gather(shift, array):
    return [array, shift(array, 1), shift(array, 2), shift(array, -1)]


def direct_scatter(shift, own, before, opposite, after):
    return [own, shift(before, -1), shift(after, 1), shift(opposite, 2)]


def on_device(tokens, w_gate, w_up, w_down, grad_output):
    tok_rows, tok_columns = tokens.shape
    rows_in, width_hidden = w_gate.shape
    own = width_hidden // 8
    width = -(-own // LANES) * LANES
    features = 8 * rows_in
    loss_scale = 1.0 / math.sqrt(tok_rows * 8)
    rows, columns = tok_rows // 2, 2 * tok_columns

    mine, theirs = local_call(split_rows, [(rows, columns)] * 2, [tokens, grad_output])
    four = [mine, swap_x_lo(theirs), swap_x_hi(mine), swap_x(theirs)]
    t_block, g_block = local_call(arrange_rows, [(2 * rows, columns)] * 2, four)

    (pieces,) = local_call(split_pair, [(8, 2 * own, rows_in)], [w_gate, w_up])
    w_near = lax.all_to_all(after(pieces, *four), "gx", 0, 0, tiled=True)
    d_near, d_far = w_down, swap_x_lo(after(w_down, *four))

    (t_own,) = local_call(
        join_features, [(2 * rows, 2 * features)], direct_gather(shift_y, t_block)
    )
    g_own = jnp.concatenate(direct_gather(shift_z, g_block), axis=0)
    t_own, g_own, w_near, d_far = lax.optimization_barrier((t_own, g_own, w_near, d_far))
    w_far = swap_x_lo(w_near)
    t_all = ring_gather(shift_z, t_own)
    g_all = ring_gather(shift_y, g_own)

    all_tokens, all_features = 8 * rows, 2 * features
    whole = (all_tokens, all_features)
    (share,) = assembled_call(
        near_products,
        [(6 * rows, 2 * own)],
        [t_all[0], t_all[1], t_all[4], w_near],
        [(6 * rows, features), (2 * own, features)],
        11,
        dtype=F32,
    )
    half_features = (all_tokens, features)
    (early,) = assembled_call(
        early_hidden_products,
        [(all_tokens, own)],
        [g_all[0], g_all[1], g_all[4], d_near, d_far],
        [(all_tokens, 3 * columns), (own, 3 * columns)],
        9,
        dtype=F32,
    )
    keep_hidden, send_hidden = assembled_call(
        hidden_products,
        [(4, rows, width)] * 2,
        [g_all[2], after(g_all[3], share), d_near, d_far, early],
        [(all_tokens, columns), (own, columns), ((all_tokens, own), F32)],
        5,
    )
    got_hidden = swap_core(send_hidden)
    weights = (2 * own, features)
    keep, send = assembled_call(
        pair_products,
        [(4, rows, 2 * width)] * 2,
        [*t_all[:4], after(t_all[4], keep_hidden), w_far, share, w_near],
        [half_features, weights, ((6 * rows, 2 * own), F32), (2 * rows, features), weights],
        24,
    )
    (mine,) = local_call(
        functools.partial(activate, own),
        [(4, rows, 3 * width)],
        [keep, swap_core(send), keep_hidden, got_hidden],
    )
    both = [mine, swap_core(mine)]

    def pair_gradient(side):
        return assembled_call(
            functools.partial(pair_gradients, loss_scale, side),
            [(8, 2 * own, rows_in)],
            [*t_all, *both],
            [half_features, (all_tokens, 2 * width)],
            13,
        )[0]

    far = pair_gradient(1)
    both[1] = after(both[1], far)
    output_parts = assembled_call(
        output_products,
        [(size * rows, all_features) for size in (2, 2, 1, 1, 2)],
        [*both, d_near, d_far],
        [(all_tokens, width), (own, all_features)],
        10,
    )
    both[1] = after(both[1], output_parts[2])
    input_parts = assembled_call(
        input_products,
        [(all_tokens, columns)] * 4,
        [*both, w_near, w_far],
        [(all_tokens, 2 * width), (2 * own, all_features)],
        24,
    )
    both[1] = after(both[1], input_parts[2])
    near = pair_gradient(0)
    down_near, down_far = assembled_call(
        functools.partial(down_gradients, loss_scale),
        [(own, features)] * 2,
        [*g_all, *both],
        [whole, (all_tokens, width)],
        18,
    )

    grad_pair = add(near, swap_x_lo(far)).astype(BF16)
    down_far = after(down_far, grad_pair)
    total = lax.all_to_all(after(grad_pair, down_near), "gx", 0, 0, tiled=True)
    grad_down = add(down_near, swap_x_lo(down_far)).astype(BF16)

    own, before, low, high, after_it = output_parts
    from_z = shift_z(low, 1), shift_z(high, -1)
    after_it = lax.dynamic_update_slice(
        after_it, add(after_it[:rows], from_z[0]).astype(BF16), (0, 0)
    )
    before = lax.dynamic_update_slice(
        before, add(before[rows:], from_z[1]).astype(BF16), (rows, 0)
    )
    output = own.astype(F32) + shift_z(after_it, 1).astype(F32)
    output = (output + shift_z(before, -1).astype(F32)).astype(BF16)
    own, before, opposite, after_it = input_parts
    from_y = shift_y(before, -1), shift_y(after_it, 1)
    opposite = after(opposite, *from_y, *from_z)
    grad_input = own.astype(F32) + from_y[0].astype(F32) + from_y[1].astype(F32)
    grad_input = (grad_input + shift_y(opposite, 2).astype(F32)).astype(BF16)
    grad_input = after(grad_input, total)
    parts = [grad_input[2 * k * rows : 2 * (k + 1) * rows] for k in range(4)]
    input_parts = direct_scatter(shift_z, *parts)
    parts = local_call(pick_features, [(2 * rows, columns)] * 4, [output])
    output_parts = direct_scatter(shift_y, *parts)
    grads = local_call(join_blocks, [(rows_in, width_hidden)] * 2, [total])
    output_parts[0], grad_down, *grads = lax.optimization_barrier(
        (output_parts[0], grad_down, *grads)
    )
    near, far, near_x, far_x = local_call(
        split_result, [(rows, columns)] * 4, [*output_parts, *input_parts]
    )
    four = [near, swap_x_hi(near_x), swap_x_lo(far), swap_x(far_x)]
    output, grad_input = local_call(join_result, [tokens.shape] * 2, four)
    return (output, grad_input, *grads, grad_down)


def solution(mesh):
    placed = (
        P("gx", ("gz", "gy")),
        P(("gz", "gx"), "gy"),
        P(("gz", "gx"), "gy"),
        P(("gy", "gx"), "gz"),
        P("gx", ("gz", "gy")),
    )
    return jax.shard_map(
        on_device,
        mesh=mesh,
        in_specs=placed,
        out_specs=(
            P("gx", ("gz", "gy")),
            P("gx", ("gz", "gy")),
            P(("gz", "gx"), "gy"),
            P(("gz", "gx"), "gy"),
            P(("gy", "gx"), "gz"),
        ),
        check_vma=False,
    )
```

```python
import functools
import math

import jax
import jax.numpy as jnp
from jax import lax
from jax.experimental import pallas as pl
from jax.experimental.pallas import tpu as pltpu
from jax.sharding import PartitionSpec as P


BF16 = jnp.bfloat16
F32 = jnp.float32
LANES = 128


def shift_z(array, steps):
    return lax.ppermute(
        array, "gx", [(i, ((i // 2 + steps) % 4) * 2 + i % 2) for i in range(8)]
    )


def shift_y(array, steps):
    return lax.ppermute(array, "gy", [(i, (i + steps) % 4) for i in range(4)])


def swap_x_hi(array):
    return lax.ppermute(array, "gx", [(i, i ^ 1) for i in range(8)])


def swap_x_lo(array):
    return lax.ppermute(array, "gz", [(i, i ^ 2) for i in range(4)])


def swap_x(array):
    return lax.ppermute(array, ("gx", "gz"), [(i, i ^ 6) for i in range(32)])


def swap_core(array):
    return lax.ppermute(array, "gz", [(i, i ^ 1) for i in range(4)])


def add(left_side, right_side):
    return left_side.astype(F32) + right_side.astype(F32)


def dot(left_side, right_side, left_dim, right_dim):
    return lax.dot_general(
        left_side,
        right_side,
        (((left_dim,), (right_dim,)), ((), ())),
        preferred_element_type=F32,
    )


class Operand:
    def __init__(self, source, held, semaphore):
        self.copy = pltpu.make_async_copy(source, held, semaphore)
        self.copy.start()
        self.held = held
        self.shape = held.shape

    def ready(self):
        if self.copy is not None:
            self.copy.wait()
            self.copy = None
        return self.held

    def __getitem__(self, index):
        return self.ready()[index]


def local_call(kernel, out_shapes, operands, scratch_shapes=(), vmem=40):
    count, outs = len(operands), len(out_shapes)

    def body(*refs):
        sources, refs = refs[:count], refs[count:]
        results, refs = refs[:outs], refs[outs:]
        held, semaphores, scratch = refs[:count], refs[count], refs[count + 1 :]
        inputs = [
            Operand(source, place, semaphores.at[i])
            for i, (source, place) in enumerate(zip(sources, held))
        ]
        kernel(*inputs, *results, *scratch)
        for operand in inputs:
            operand.ready()

    return list(
        pl.pallas_call(
            body,
            out_shape=[jax.ShapeDtypeStruct(shape, BF16) for shape in out_shapes],
            in_specs=[pl.BlockSpec(memory_space=pl.ANY)] * count,
            out_specs=[pl.BlockSpec(memory_space=pltpu.VMEM)] * outs,
            scratch_shapes=[
                *(pltpu.VMEM(array.shape, BF16) for array in operands),
                pltpu.SemaphoreType.DMA((count,)),
                *scratch_shapes,
            ],
            compiler_params=pltpu.CompilerParams(vmem_limit_bytes=vmem * 2**20),
        )(*operands)
    )


def assembled_call(kernel, out_shapes, operands, buffers, copies, vmem=40, dtype=BF16):
    count, outs = len(operands), len(out_shapes)
    buffers = [buffer if len(buffer) == 2 and isinstance(buffer[0], tuple) else (buffer, BF16) for buffer in buffers]

    def body(*refs):
        sources, refs = refs[:count], refs[count:]
        results, (*held, semaphores) = refs[:outs], refs[outs:]
        started = []

        def copy(source, target):
            started.append(pltpu.make_async_copy(source, target, semaphores.at[len(started)]))
            started[-1].start()
            return started[-1]

        kernel(copy, sources, results, *held)

    return list(
        pl.pallas_call(
            body,
            out_shape=[jax.ShapeDtypeStruct(shape, dtype) for shape in out_shapes],
            in_specs=[pl.BlockSpec(memory_space=pl.ANY)] * count,
            out_specs=[pl.BlockSpec(memory_space=pltpu.VMEM)] * outs,
            scratch_shapes=[
                *(pltpu.VMEM(*buffer) for buffer in buffers),
                pltpu.SemaphoreType.DMA((copies,)),
            ],
            compiler_params=pltpu.CompilerParams(vmem_limit_bytes=vmem * 2**20),
        )(*operands)
    )


def wait_all(copies):
    for copy in copies:
        copy.wait()


def after(array, *earlier):
    return lax.optimization_barrier((array, *earlier))[0]


def core_index():
    return lax.rem(lax.axis_index("gz"), 2)


def x_lo_index():
    return lax.div(lax.axis_index("gz"), 2)


def block(index, count):
    return pl.ds(pl.multiple_of(index * count, count), count)


def feature_block(k, count):
    return block(lax.rem(lax.axis_index("gy") + (4 - k), 4), count)


def split_rows(tokens, grads, mine, theirs):
    half, count = mine.shape[0], tokens.shape[1]
    for out, index in ((mine, x_lo_index()), (theirs, 1 - x_lo_index())):
        out[:, :count] = tokens[block(index, half)]
        out[:, count:] = grads[block(index, half)]


def arrange_rows(near, far, near_x, far_x, tokens, grads):
    half, count = near.shape[0], near.shape[1] // 2
    core = core_index()
    for index, left, right in ((core, near, far), (1 - core, near_x, far_x)):
        tokens[block(index, half), :count] = left[:, :count]
        tokens[block(index, half), count:] = right[:, :count]
        grads[block(index, half), :count] = left[:, count:]
        grads[block(index, half), count:] = right[:, count:]


def split_pair(w_gate, w_up, out):
    groups, own = out.shape[0], out.shape[1] // 2
    for first, array in ((0, w_gate), (own, w_up)):
        for g in range(groups):
            out[g, first : first + own] = array[:, g * own : (g + 1) * own].T


def join_blocks(pieces, gate, up):
    groups, both, _ = pieces.shape
    own = both // 2
    for g in range(groups):
        gate[:, g * own : (g + 1) * own] = pieces[g, :own].T
        up[:, g * own : (g + 1) * own] = pieces[g, own:].T


def join_features(*refs):
    *blocks, out = refs
    count, features = blocks[0].shape[1] // 2, out.shape[1] // 2
    for k, part in enumerate(blocks):
        place = lax.rem(lax.axis_index("gy") + (4 - k), 4) * count
        out[:, pl.ds(pl.multiple_of(place, count), count)] = part[:, :count]
        out[:, pl.ds(pl.multiple_of(features + place, count), count)] = part[:, count:]


def pick_features(whole, *outs):
    count, features = outs[0].shape[1] // 2, whole.shape[1] // 2
    for k, out in enumerate(outs):
        place = lax.rem(lax.axis_index("gy") + (4 - k), 4) * count
        out[:, :count] = whole[:, pl.ds(pl.multiple_of(place, count), count)]
        out[:, count:] = whole[:, pl.ds(pl.multiple_of(features + place, count), count)]


def own_place(k, count):
    return lax.rem(lax.axis_index("gy") + (4 - k), 4) * count


def copy_tokens(copy, refs, held):
    copies, first = [], 0
    for ref in refs:
        copies.append(copy(ref, held.at[pl.ds(first, ref.shape[0])]))
        first += ref.shape[0]
    return copies


def copy_grads(copy, refs, held):
    copies = []
    count, features = refs[0].shape[1] // 2, held.shape[1] // 2
    for ref, k, first in zip(refs, (0, 1, 2, 2, 3), (0, 0, 0, refs[2].shape[0], 0)):
        for side in (0, 1):
            place = side * features + own_place(k, count)
            target = held.at[
                pl.ds(first, ref.shape[0]), pl.ds(pl.multiple_of(place, count), count)
            ]
            copies.append(copy(ref.at[:, pl.ds(side * count, count)], target))
    return copies


def copy_blocks(copy, ref, held):
    groups, _, count = ref.shape
    return [copy(ref.at[g], held.at[:, pl.ds(g * count, count)]) for g in range(groups)]


def copy_pair(copy, near, far, held):
    features = held.shape[1] // 2
    copies = copy_blocks(copy, near, held.at[:, pl.ds(0, features)])
    return copies + copy_blocks(copy, far, held.at[:, pl.ds(features, features)])


def copy_down(copy, near, far, held):
    features = near.shape[1]
    return [
        copy(ref, held.at[:, pl.ds(side * features, features)])
        for side, ref in enumerate((near, far))
    ]


def copy_part(copy, mine, other, first, held):
    rows, width = mine.shape[1], held.shape[1]
    return [
        copy(
            ref.at[i, :, pl.ds(first, width)], held.at[pl.ds((2 * i + side) * rows, rows)]
        )
        for i in range(mine.shape[0])
        for side, ref in enumerate((mine, other))
    ]


def near_products(copy, sources, results, tokens, pair):
    features = tokens.shape[1]
    copies = copy_blocks(copy, sources[3], pair)
    copies += copy_tokens(copy, [ref.at[:, pl.ds(0, features)] for ref in sources[:3]], tokens)
    wait_all(copies)
    results[0][...] = dot(tokens[...], pair[...], 1, 1)


def pair_products(copy, sources, results, tokens, pair, share, opposite, near):
    keep, send = results
    half, width = keep.shape[1], keep.shape[2] // 2
    own = pair.shape[0] // 2
    features = tokens.shape[1]
    copies = copy_blocks(copy, sources[5], pair)
    chunks = copy_tokens(
        copy, [ref.at[:, pl.ds(features, features)] for ref in sources[:5]], tokens
    )
    chunks.append(copy(sources[6], share))
    later = copy_blocks(copy, sources[7], near)
    later += copy_tokens(
        copy, [ref.at[:, pl.ds(0, features)] for ref in sources[2:4]], opposite
    )
    wait_all(copies + chunks)
    padding = jnp.zeros((half, width - own), BF16)
    for i in (0, 2):
        part = dot(tokens[pl.ds(2 * i * half, 4 * half)], pair[...], 1, 1)
        if i == 0:
            part = part + share[pl.ds(0, 4 * half)]
        else:
            wait_all(later)
            first = part[: 2 * half] + dot(opposite[...], near[...], 1, 1)
            part = jnp.concatenate([first, part[2 * half :] + share[pl.ds(4 * half, 2 * half)]])
        part = part.astype(BF16)
        for j in (0, 1):
            for out, at in ((keep, 2 * j * half), (send, (2 * j + 1) * half)):
                piece = part[at : at + half]
                for k in (0, 1):
                    out[i + j, :, k * width : k * width + own] = piece[:, k * own : (k + 1) * own]
                    out[i + j, :, k * width + own : (k + 1) * width] = padding


def copy_down_blocks(copy, near, far, blocks, held):
    count = held.shape[1] // (2 * len(blocks))
    return [
        copy(
            ref.at[:, feature_block(k, count)],
            held.at[:, pl.ds((2 * i + side) * count, count)],
        )
        for i, k in enumerate(blocks)
        for side, ref in enumerate((near, far))
    ]


def early_hidden_products(copy, sources, results, grads, down):
    columns = sources[0].shape[1]
    copies = copy_down_blocks(copy, *sources[3:], (0, 1, 3), down)
    copies += [
        copy(ref, grads.at[:, pl.ds(i * columns, columns)]) for i, ref in enumerate(sources[:3])
    ]
    wait_all(copies)
    results[0][...] = dot(grads[...], down[...], 1, 1)


def hidden_products(copy, sources, results, grads, down, share):
    keep, send = results
    half, width = keep.shape[1:]
    own = down.shape[0]
    copies = copy_down_blocks(copy, *sources[2:4], (2,), down)
    copies += copy_tokens(copy, sources[:2], grads)
    wait_all(copies + [copy(sources[4], share)])
    padding = jnp.zeros((half, width - own), BF16)
    for i in (0, 2):
        here = pl.ds(2 * i * half, 4 * half)
        part = (dot(grads[here], down[...], 1, 1) + share[here]).astype(BF16)
        for j in (0, 1):
            for out, at in ((keep, 2 * j * half), (send, (2 * j + 1) * half)):
                out[i + j, :, :own] = part[at : at + half]
                out[i + j, :, own:] = padding


def activate(own, keep, got, keep_hidden, got_hidden, out):
    width = out.shape[2] // 3
    padding = jnp.zeros((out.shape[1], 3 * width - (width + 2 * own)), BF16)
    for i in range(out.shape[0]):
        gate_sum, up_sum = (
            add(keep[i, :, k * width : (k + 1) * width], got[i, :, k * width : (k + 1) * width])
            for k in range(2)
        )
        grad_hidden = add(keep_hidden[i], got_hidden[i])
        sigmoid_gate = jax.nn.sigmoid(gate_sum)
        out[i, :, :width] = (gate_sum * sigmoid_gate * up_sum).astype(BF16)
        grad_gate_act = grad_hidden * up_sum * sigmoid_gate * (1.0 + gate_sum * (1.0 - sigmoid_gate))
        out[i, :, width : 2 * width] = grad_gate_act.astype(BF16)
        grad_up_act = (grad_hidden * gate_sum * sigmoid_gate).astype(BF16)
        out[i, :, width + own : width + 2 * own] = grad_up_act[:, :own]
        out[i, :, width + 2 * own :] = padding


def output_products(copy, sources, results, hidden, down):
    copies = copy_part(copy, sources[0], sources[1], 0, hidden)
    wait_all(copies + copy_down(copy, *sources[2:], down))
    own, first = down.shape[0], 0
    for out in results:
        rows = out.shape[0]
        out[...] = dot(hidden[pl.ds(first, rows), :own], down[...], 1, 0).astype(BF16)
        first += rows


def input_products(copy, sources, results, acts, pair):
    copies = copy_part(copy, sources[0], sources[1], acts.shape[1] // 2, acts)
    wait_all(copies + copy_pair(copy, *sources[2:], pair))
    both = pair.shape[0]
    count, features = results[0].shape[1] // 2, pair.shape[1] // 2
    for k, out in enumerate(results):
        for side in (0, 1):
            place = pl.ds(pl.multiple_of(side * features + own_place(k, count), count), count)
            part = dot(acts[:, :both], pair[:, place], 1, 0)
            out[:, side * count : (side + 1) * count] = part.astype(BF16)


def pair_gradients(scale, side, copy, sources, results, tokens, acts):
    groups, both, count = results[0].shape
    features = groups * count
    columns = [ref.at[:, pl.ds(side * features, features)] for ref in sources[:5]]
    copies = copy_tokens(copy, columns, tokens)
    wait_all(copies + copy_part(copy, *sources[5:], acts.shape[1] // 2, acts))
    total = dot(acts[:, :both], tokens[...], 0, 0) * scale
    for g in range(groups):
        results[0][g] = total[:, g * count : (g + 1) * count].astype(BF16)


def down_gradients(scale, copy, sources, results, grads, hidden):
    copies = copy_grads(copy, sources[:5], grads)
    wait_all(copies + copy_part(copy, *sources[5:], 0, hidden))
    near, far = results
    own, features = near.shape
    for out, first in ((far, features), (near, 0)):
        total = dot(hidden[:, :own], grads[:, pl.ds(first, features)], 0, 0)
        out[...] = (total * scale).astype(BF16)


def split_result(*refs):
    *parts, near, far, near_x, far_x = refs
    half, count = near.shape[0], near.shape[1] // 2
    core = core_index()
    for first, arrays in ((0, parts[:4]), (count, parts[4:])):
        for index, left, right in ((core, near, far), (1 - core, near_x, far_x)):
            rows = sum(array[block(index, half)].astype(F32) for array in arrays).astype(BF16)
            left[:, first : first + count] = rows[:, :count]
            right[:, first : first + count] = rows[:, count:]


def join_result(near, near_x, far, far_x, output, grad_input):
    half, count = near.shape[0], near.shape[1] // 2
    for parts, index in (((near, near_x), x_lo_index()), ((far, far_x), 1 - x_lo_index())):
        rows = add(parts[0][...], parts[1][...]).astype(BF16)
        output[block(index, half)] = rows[:, :count]
        grad_input[block(index, half)] = rows[:, count:]


def ring_gather(shift, array):
    half = array.shape[0] // 2
    before, after = shift(array, 1), shift(array, -1)
    return [array, before, shift(before[:half], 1), shift(after[half:], -1), after]


def direct_gather(shift, array):
    return [array, shift(array, 1), shift(array, 2), shift(array, -1)]


def direct_scatter(shift, own, before, opposite, after):
    return [own, shift(before, -1), shift(after, 1), shift(opposite, 2)]


def on_device(tokens, w_gate, w_up, w_down, grad_output):
    tok_rows, tok_columns = tokens.shape
    rows_in, width_hidden = w_gate.shape
    own = width_hidden // 8
    width = -(-own // LANES) * LANES
    features = 8 * rows_in
    loss_scale = 1.0 / math.sqrt(tok_rows * 8)
    rows, columns = tok_rows // 2, 2 * tok_columns

    mine, theirs = local_call(split_rows, [(rows, columns)] * 2, [tokens, grad_output], vmem=58)
    four = [mine, swap_x_lo(theirs), swap_x_hi(mine), swap_x(theirs)]
    t_block, g_block = local_call(arrange_rows, [(2 * rows, columns)] * 2, four)

    (pieces,) = local_call(split_pair, [(8, 2 * own, rows_in)], [w_gate, w_up], vmem=58)
    w_near = lax.all_to_all(after(pieces, *four), "gx", 0, 0, tiled=True)
    d_near, d_far = w_down, swap_x_lo(after(w_down, *four))

    (t_own,) = local_call(
        join_features, [(2 * rows, 2 * features)], direct_gather(shift_y, t_block)
    )
    g_own = jnp.concatenate(direct_gather(shift_z, g_block), axis=0)
    t_own, g_own, w_near, d_far = lax.optimization_barrier((t_own, g_own, w_near, d_far))
    w_far = swap_x_lo(w_near)
    t_all = ring_gather(shift_z, t_own)
    g_all = ring_gather(shift_y, g_own)

    all_tokens, all_features = 8 * rows, 2 * features
    whole = (all_tokens, all_features)
    (share,) = assembled_call(
        near_products,
        [(6 * rows, 2 * own)],
        [t_all[0], t_all[1], t_all[4], w_near],
        [(6 * rows, features), (2 * own, features)],
        11,
        dtype=F32,
    )
    half_features = (all_tokens, features)
    (early,) = assembled_call(
        early_hidden_products,
        [(all_tokens, own)],
        [g_all[0], g_all[1], g_all[4], d_near, d_far],
        [(all_tokens, 3 * columns), (own, 3 * columns)],
        9,
        dtype=F32,
    )
    keep_hidden, send_hidden = assembled_call(
        hidden_products,
        [(4, rows, width)] * 2,
        [g_all[2], after(g_all[3], share), d_near, d_far, early],
        [(all_tokens, columns), (own, columns), ((all_tokens, own), F32)],
        5,
    )
    got_hidden = swap_core(send_hidden)
    weights = (2 * own, features)
    keep, send = assembled_call(
        pair_products,
        [(4, rows, 2 * width)] * 2,
        [*t_all[:4], after(t_all[4], keep_hidden), w_far, share, w_near],
        [half_features, weights, ((6 * rows, 2 * own), F32), (2 * rows, features), weights],
        24,
    )
    (mine,) = local_call(
        functools.partial(activate, own),
        [(4, rows, 3 * width)],
        [keep, swap_core(send), keep_hidden, got_hidden],
    )
    both = [mine, swap_core(mine)]

    def pair_gradient(side):
        return assembled_call(
            functools.partial(pair_gradients, loss_scale, side),
            [(8, 2 * own, rows_in)],
            [*t_all, *both],
            [half_features, (all_tokens, 2 * width)],
            13,
        )[0]

    far = pair_gradient(1)
    both[1] = after(both[1], far)
    output_parts = assembled_call(
        output_products,
        [(size * rows, all_features) for size in (2, 2, 1, 1, 2)],
        [*both, d_near, d_far],
        [(all_tokens, width), (own, all_features)],
        10,
    )
    both[1] = after(both[1], output_parts[2])
    input_parts = assembled_call(
        input_products,
        [(all_tokens, columns)] * 4,
        [*both, w_near, w_far],
        [(all_tokens, 2 * width), (2 * own, all_features)],
        24,
    )
    both[1] = after(both[1], input_parts[2])
    near = pair_gradient(0)
    down_near, down_far = assembled_call(
        functools.partial(down_gradients, loss_scale),
        [(own, features)] * 2,
        [*g_all, *both],
        [whole, (all_tokens, width)],
        18,
    )

    grad_pair = add(near, swap_x_lo(far)).astype(BF16)
    down_far = after(down_far, grad_pair)
    total = lax.all_to_all(after(grad_pair, down_near), "gx", 0, 0, tiled=True)
    grad_down = add(down_near, swap_x_lo(down_far)).astype(BF16)

    own, before, low, high, after_it = output_parts
    from_z = shift_z(low, 1), shift_z(high, -1)
    after_it = lax.dynamic_update_slice(
        after_it, add(after_it[:rows], from_z[0]).astype(BF16), (0, 0)
    )
    before = lax.dynamic_update_slice(
        before, add(before[rows:], from_z[1]).astype(BF16), (rows, 0)
    )
    output = own.astype(F32) + shift_z(after_it, 1).astype(F32)
    output = (output + shift_z(before, -1).astype(F32)).astype(BF16)
    own, before, opposite, after_it = input_parts
    from_y = shift_y(before, -1), shift_y(after_it, 1)
    opposite = after(opposite, *from_y, *from_z)
    grad_input = own.astype(F32) + from_y[0].astype(F32) + from_y[1].astype(F32)
    grad_input = (grad_input + shift_y(opposite, 2).astype(F32)).astype(BF16)
    grad_input = after(grad_input, total)
    parts = [grad_input[2 * k * rows : 2 * (k + 1) * rows] for k in range(4)]
    input_parts = direct_scatter(shift_z, *parts)
    parts = local_call(pick_features, [(2 * rows, columns)] * 4, [output])
    output_parts = direct_scatter(shift_y, *parts)
    grads = local_call(join_blocks, [(rows_in, width_hidden)] * 2, [total])
    output_parts[0], grad_down, *grads = lax.optimization_barrier(
        (output_parts[0], grad_down, *grads)
    )
    near, far, near_x, far_x = local_call(
        split_result, [(rows, columns)] * 4, [*output_parts, *input_parts]
    )
    four = [near, swap_x_hi(near_x), swap_x_lo(far), swap_x(far_x)]
    output, grad_input = local_call(join_result, [tokens.shape] * 2, four)
    return (output, grad_input, *grads, grad_down)


def solution(mesh):
    placed = (
        P("gx", ("gz", "gy")),
        P(("gz", "gx"), "gy"),
        P(("gz", "gx"), "gy"),
        P(("gy", "gx"), "gz"),
        P("gx", ("gz", "gy")),
    )
    return jax.shard_map(
        on_device,
        mesh=mesh,
        in_specs=placed,
        out_specs=(
            P("gx", ("gz", "gy")),
            P("gx", ("gz", "gy")),
            P(("gz", "gx"), "gy"),
            P(("gz", "gx"), "gy"),
            P(("gy", "gx"), "gz"),
        ),
        check_vma=False,
    )
```
